32 devices in a mesh: grp: 4 (over z), dev: 8 (over y, x, core).
Axes of the slice: x: 2, y: 2, z: 4, core: 2. Of those that a mesh axis runs over, the one named last changes fastest.
Arguments:
- head_emb: bfloat16 [32768, 400], P(('grp', 'dev')), may hold values from -2 to 2
- tail_emb: bfloat16 [32768, 400], P(('grp', 'dev')), may hold values from -2 to 2
- relation: int32 [32768], P(('grp', 'dev')), may hold values from 0 to 14823
- owners: int32 [32768, 2], P(('grp', 'dev')), may hold values from 0 to 31, all different within a row; in each aligned block of 1024 rows (0 to 1023, 1024 to 2047, ...) at most 128 rows name the same one
- owner_rows: int32 [32768, 2], P(('grp', 'dev')), may hold values from 0 to 4095
- entities: bfloat16 [131072, 400], P(('grp', 'dev')), may hold values from -2 to 2
- neg_rows: int32 [1, 4096], P(None, ('grp', 'dev')), may hold values from 0 to 4095
- coef: float32 [14824, 100], replicated, may hold values from -4 to 4
- bases: float32 [100, 400], replicated, may hold values from -0.625 to 0.625
Outputs:
- ent_grad: float32 [131072, 400], P(('grp', 'dev'))
- coef_grad: float32 [14824, 100], replicated
- bases_grad: float32 [100, 400], replicated
The draws below stay inside these ranges and needn't reach their ends.
Inputs may be any that keep to these rules, and one draw needn't show every extreme that they name: The two owners of a row differ; within the triples of one device no owner is named by more than 128 entries of both columns together.
All inputs are finite; a program needn't handle non-finite values.
Results may differ from the reference program's by a relative error of at most 0.0029.
Values may be sent and summed in bfloat16 or wider, within the bound.
No kernel may reach another device: no remote copies, remote signals or barrier semaphores. Data moves between devices by JAX's collectives and lax.ppermute only.
A program may use at most 128 MiB of HBM per device.

```python
import math
import jax
import jax.numpy as jnp
import numpy as np
from jax import lax

D = 400
NREL = 14824
NB = 100
BLOCK = 1024
TRIP_DEV = 1024
NEG_DEV = 128
ENT_DEV = 4096
BLOCKS = 1
CAP = 128
TRIPLES = 32768
NENT = 131072
N_GRP = 4
N_DEV = 8
DEVICES = 32


def touch_ends(entries, key, low, top_value):
    spot = [jax.random.randint(jax.random.fold_in(key, axis), (), 0, length) for axis, length in enumerate(entries.shape)]
    widest = entries.shape.index(max(entries.shape))
    beside = spot[:widest] + [(spot[widest] + 1) % entries.shape[widest]] + spot[widest + 1:]
    return entries.at[tuple(spot)].set(low).at[tuple(beside)].set(top_value)


def levels(rng, dims, split, smallest, largest):
    level = 1.0
    for axis_at, parts in split:
        heights = jax.random.uniform(jax.random.fold_in(jax.random.fold_in(rng, 6), axis_at), (parts,), jnp.float32, smallest / len(split), largest / len(split))
        level = level * jnp.repeat(jnp.exp(heights), dims[axis_at] // parts).reshape((-1,) + (1,) * (len(dims) - 1 - axis_at))
    return level


def rank_bounds(count, lean):
    portions = [(1 << 20) // math.isqrt(rank ** lean) + 1 for rank in range(1, count + 1)]
    spread = 1 + sum(portions) // (1 << 30)
    return np.cumsum(np.array([max(1, weight // spread) for weight in portions]))


def ranked_ids(stream_key, extent, amount, skew):
    grid = rank_bounds(amount, skew)
    ticket = jax.random.randint(jax.random.fold_in(stream_key, 1), extent, 0, int(grid[amount - 1]))
    rank = jnp.searchsorted(jnp.asarray(grid, jnp.int32), ticket, side="right")
    return jax.random.permutation(jax.random.fold_in(stream_key, 2), amount)[rank].astype(jnp.int32)


def deal_out(stream_key, own, number, rows, count, top, reach, slope):
    sequence = jax.random.permutation(stream_key, count)
    crowded, ordinary = shares(count, rows * top, reach, slope, True), shares(count, rows * top, reach, slope, False)
    places = jnp.arange(count)

    def named(tallies, turn):
        used = int((tallies > 0).sum())
        fixed = max(1, used // 4)
        shifted = fixed + (places - fixed + turn * (used - fixed)) % max(1, count - fixed)
        return jnp.zeros((count,), jnp.int32).at[sequence[jnp.where(places < fixed, places, shifted)]].set(jnp.asarray(tallies, jnp.int32))

    tallies = jnp.where(number % 4 == 0, named(crowded, number // 4), named(ordinary, number - number // 4 - 1))
    mixed = jax.random.permutation(jax.random.fold_in(own, 3), count)
    giver, taker = mixed[0:count // 2 * 2:2], mixed[1:count // 2 * 2:2]
    margin = jnp.minimum(tallies[giver] - 1, reach - tallies[taker]) // 2
    margin = jnp.where((giver == sequence[0]) | (taker == sequence[0]) | (tallies[taker] == 0), 0, jnp.maximum(margin, 0))
    shifted = jax.random.randint(jax.random.fold_in(own, 4), (count // 2,), 0, 1 << 20) % (margin + 1)
    tallies = tallies.at[giver].add(-shifted).at[taker].add(shifted)
    items = jnp.searchsorted(jnp.cumsum(tallies), jnp.arange(rows * top), side="right").astype(jnp.int32)
    listing = items.reshape(top, rows).T
    listing = listing[jax.random.permutation(jax.random.fold_in(own, 1), rows)]
    turn = jax.random.randint(jax.random.fold_in(own, 2), (rows, 1), 0, top)
    return jnp.take_along_axis(listing, (jnp.arange(top)[None, :] + turn) % top, axis=1)


def shares(amount, total, reach, skew, full):
    portions = [(1 << 20) // math.isqrt(grade ** skew) + 1 for grade in range(1, amount + 1)]
    largest = reach if full else min(reach, max(-(-total // amount), total * portions[0] // sum(portions)))
    least = 1 if total - largest >= amount - 1 else 0
    given, spare = [largest] + [least] * (amount - 1), total - largest - least * (amount - 1)
    while spare > 0:
        candidates = [i for i in range(1, amount) if given[i] < largest] or [i for i in range(1, amount) if given[i] < reach]
        whole, remaining = sum([portions[i] for i in candidates]), spare
        for i in candidates:
            addition = min(reach - given[i], max(1, remaining * portions[i] // whole), spare)
            given[i] = given[i] + addition
            spare = spare - addition
    return np.array(given)


def scatter_about(key, shape, scale, bound, split=(), kind=jnp.bfloat16):
    array = scale * jax.random.normal(key, shape, jnp.float32)
    if split:
        array = array * levels(key, shape, split, -0.22, 0.18)
    return jnp.clip(array, -bound, bound).astype(kind)


def setup_inputs(seed: int = 0) -> dict:
    key_of = jax.random.split(jax.random.key(seed), 10)
    head_emb = scatter_about(key_of[0], (TRIPLES, D), 0.3, 2.0, ((0, 32),))
    tail_emb = scatter_about(key_of[1], (TRIPLES, D), 0.3, 2.0, ((0, 32),))
    relation = touch_ends(ranked_ids(key_of[2], (TRIPLES,), NREL, 2), jax.random.fold_in(key_of[2], 3), 0, NREL - 1).astype(jnp.int32)
    owners_keys = jax.random.split(jax.random.fold_in(key_of[3], 1), TRIPLES // TRIP_DEV)
    owners_turns = jax.random.permutation(jax.random.fold_in(key_of[3], 3), TRIPLES // TRIP_DEV)
    owners = jax.vmap(lambda own, number: deal_out(jax.random.fold_in(key_of[3], 2), own, number, TRIP_DEV, DEVICES, 2, CAP, 2))(owners_keys, owners_turns).reshape((TRIPLES, 2))
    owner_rows = touch_ends(jax.random.randint(key_of[4], (TRIPLES, 2), 0, ENT_DEV), jax.random.fold_in(key_of[4], 1), 0, ENT_DEV - 1).astype(jnp.int32)
    entities = scatter_about(key_of[5], (NENT, D), 0.3, 2.0, ((0, 32),))
    neg_rows = touch_ends(jax.random.randint(key_of[6], (BLOCKS, NEG_DEV * DEVICES), 0, ENT_DEV), jax.random.fold_in(key_of[6], 1), 0, ENT_DEV - 1).astype(jnp.int32)
    coef = scatter_about(key_of[7], (NREL, NB), 1.0, 4.0, (), jnp.float32)
    bases = scatter_about(key_of[8], (NB, D), NB ** -0.5, 0.625, (), jnp.float32)
    return dict(head_emb=head_emb, tail_emb=tail_emb, relation=relation, owners=owners, owner_rows=owner_rows, entities=entities, neg_rows=neg_rows, coef=coef, bases=bases)


def score_block(packed, entities, coef, bases):
    head_blk, tail_blk, rel_blk, neg_ids = packed
    highest = lax.Precision.HIGHEST
    neg_count = NEG_DEV * N_DEV
    picked = coef[rel_blk]
    rel_vec = jnp.dot(picked, bases, precision=highest)
    negatives = entities[neg_ids]
    head_f = head_blk.astype(jnp.float32)
    tail_f = tail_blk.astype(jnp.float32)
    head_rel = (head_f * rel_vec).astype(jnp.bfloat16)
    neg_prob = jax.nn.sigmoid(jnp.dot(head_rel, negatives.T, preferred_element_type=jnp.float32)).astype(jnp.bfloat16)
    neg_mix = jnp.dot(neg_prob, negatives, preferred_element_type=jnp.float32)
    neg_grad = jnp.dot(neg_prob.T, head_rel, preferred_element_type=jnp.float32) / neg_count
    pos_gate = jax.nn.sigmoid(-jnp.sum(head_f * rel_vec * tail_f, axis=1))[:, None]
    head_grad = (-pos_gate * rel_vec * tail_f + rel_vec * neg_mix / neg_count).astype(jnp.bfloat16)
    tail_grad = (-pos_gate * head_f * rel_vec).astype(jnp.bfloat16)
    rel_grad = -pos_gate * head_f * tail_f + head_f * neg_mix / neg_count
    coef_rows = jnp.dot(rel_grad, bases.T, precision=highest)
    bases_part = jnp.dot(picked.T, rel_grad, precision=highest)
    return head_grad, tail_grad, neg_grad, coef_rows, bases_part


def reference(head_emb, tail_emb, relation, owners, owner_rows, entities, neg_rows, coef, bases):
    all_devices = N_GRP * N_DEV
    neg_count = NEG_DEV * N_DEV
    block_count = TRIP_DEV // BLOCK
    source_dev = (jnp.arange(all_devices * NEG_DEV) // NEG_DEV).astype(jnp.int32)
    neg_ids = (source_dev[None, :] * ENT_DEV + neg_rows).astype(jnp.int32)
    neg_ids = neg_ids.reshape(block_count, N_GRP, neg_count).transpose(1, 0, 2).reshape(N_GRP * block_count, neg_count)

    def arrange(values):
        tail_shape = values.shape[1:]
        shaped = values.reshape((N_GRP, N_DEV, block_count, BLOCK) + tail_shape)
        order = (0, 2, 1, 3) + tuple(range(4, 4 + len(tail_shape)))
        return shaped.transpose(order).reshape((N_GRP * block_count, N_DEV * BLOCK) + tail_shape)

    def restore(values):
        tail_shape = values.shape[2:]
        shaped = values.reshape((N_GRP, block_count, N_DEV, BLOCK) + tail_shape)
        order = (0, 2, 1, 3) + tuple(range(4, 4 + len(tail_shape)))
        return shaped.transpose(order).reshape((N_GRP * N_DEV * TRIP_DEV,) + tail_shape)

    rel_arranged = arrange(relation)
    packed = (arrange(head_emb), arrange(tail_emb), rel_arranged, neg_ids)
    head_grad, tail_grad, neg_grad, coef_rows, bases_part = lax.map(
        lambda item: score_block(item, entities, coef, bases), packed)
    head_grad = restore(head_grad)
    tail_grad = restore(tail_grad)
    target = (owners * ENT_DEV + owner_rows).astype(jnp.int32).reshape(-1)
    grad_rows = jnp.stack([head_grad, tail_grad], axis=1).astype(jnp.float32).reshape(-1, D)
    ent_grad = jnp.zeros((N_GRP * N_DEV * ENT_DEV, D), jnp.float32)
    ent_grad = ent_grad.at[target].add(grad_rows)
    ent_grad = ent_grad.at[neg_ids.reshape(-1)].add(neg_grad.reshape(-1, D))
    coef_grad = jax.ops.segment_sum(coef_rows.reshape(-1, NB), rel_arranged.reshape(-1), num_segments=NREL)
    bases_grad = jnp.sum(bases_part, axis=0)
    return ent_grad, coef_grad, bases_grad
```

```python
import functools

import jax
import jax.numpy as jnp
from jax import lax
from jax.experimental import pallas as pl
from jax.experimental.pallas import tpu as pltpu
from jax.sharding import PartitionSpec as P

F32, BF16, I32 = jnp.float32, jnp.bfloat16, jnp.int32
HIGHEST = lax.Precision.HIGHEST
LANES = 128
PAD = 112
VMEM_BYTES = 56 * 1024 * 1024


def nt(a, b, **kw):
    return lax.dot_general(a, b, (((1,), (1,)), ((), ())), preferred_element_type=F32, **kw)


def tn(a, b, **kw):
    return lax.dot_general(a, b, (((0,), (0,)), ((), ())), preferred_element_type=F32, **kw)


def nn(a, b, **kw):
    return lax.dot_general(a, b, (((1,), (0,)), ((), ())), preferred_element_type=F32, **kw)


def params():
    return pltpu.CompilerParams(vmem_limit_bytes=VMEM_BYTES)


def cost(flops, nbytes):
    return pl.CostEstimate(flops=flops, bytes_accessed=nbytes, transcendentals=0)


def hits(ids, rows, first):
    row = lax.broadcasted_iota(I32, (rows, ids.shape[1]), 0)
    return jnp.where(row == ids - first, 1.0, 0.0).astype(BF16)


def pick_negs_kernel(ids_ref, ent_ref, out_ref, acc_ref):
    step = pl.program_id(0)
    width = ent_ref.shape[1]
    part = nn(ent_ref[...], hits(ids_ref[...], width, step * width))

    @pl.when(step == 0)
    def _():
        acc_ref[...] = part

    @pl.when(step > 0)
    def _():
        acc_ref[...] += part

    @pl.when(step == pl.num_programs(0) - 1)
    def _():
        rows = acc_ref[...].astype(BF16)
        for k in range(out_ref.shape[0]):
            out_ref[k] = rows


def pick_negs(ids, ent_t, group):
    cols, ent = ent_t.shape
    width = 1024
    return pl.pallas_call(
        pick_negs_kernel,
        grid=(ent // width,),
        in_specs=[
            pl.BlockSpec((1, ids.shape[1]), lambda i: (0, 0)),
            pl.BlockSpec((cols, width), lambda i: (0, i)),
        ],
        out_specs=pl.BlockSpec((group, cols, ids.shape[1]), lambda i: (0, 0, 0)),
        out_shape=jax.ShapeDtypeStruct((group, cols, ids.shape[1]), BF16),
        scratch_shapes=[pltpu.VMEM((cols, ids.shape[1]), F32)],
        compiler_params=params(),
        cost_estimate=cost(2 * cols * ent * 128, cols * ent * 2),
        name="pick_negs",
    )(ids, ent_t)


def relation_kernel(nrel, devices, cap, rel_ref, coef_ref, bases_ref, head_ref, tail_ref,
                    owner_ref, picked_ref, vec_ref, gate_ref, tgrad_ref, pos_ref, halves, acc):
    step = pl.program_id(0)
    width = coef_ref.shape[1]
    nb = coef_ref.shape[0]
    lane = lax.broadcasted_iota(I32, (nb, width), 1) + step * width
    block = jnp.where(lane < nrel, coef_ref[...], 0.0)
    high = block.astype(BF16)

    @pl.when(step == 0)
    def _():
        acc[...] = jnp.zeros_like(acc)

    low = block - high.astype(F32)
    spare = jnp.zeros((PAD - nb, width), F32)
    halves[0:PAD] = jnp.concatenate([block, spare], axis=0).astype(BF16)
    halves[PAD:] = jnp.concatenate([low, spare], axis=0).astype(BF16)
    acc[...] += nn(halves[...], hits(rel_ref[...], width, step * width))

    @pl.when(step == pl.num_programs(0) - 1)
    def _():
        picked = acc[0:nb] + acc[PAD:PAD + nb]
        picked_ref[...] = picked
        vec = nn(bases_ref[...], picked, precision=HIGHEST)
        vec_ref[...] = vec
        head = head_ref[...].astype(F32)
        head_vec = head * vec
        score = jnp.sum(head_vec * tail_ref[...].astype(F32), axis=0, keepdims=True)
        gate = jax.nn.sigmoid(-score)
        gate_ref[...] = gate
        tgrad_ref[...] = (-gate * head * vec).astype(BF16)
        owner = owner_ref[...]
        triples = owner.shape[1]
        rows = lax.broadcasted_iota(I32, (LANES, LANES), 0)
        cols = lax.broadcasted_iota(I32, (LANES, LANES), 1)
        upto = jnp.where(rows <= cols, 1.0, 0.0).astype(BF16)
        number = lax.broadcasted_iota(I32, (devices, LANES), 0)
        owners, marks = [], []
        for side in range(2):
            for b in range(triples // LANES):
                o = owner[side:side + 1, b * LANES:(b + 1) * LANES]
                owners.append(o)
                marks.append(jnp.where(number == o, 1.0, 0.0))
        sums = nn(jnp.concatenate(marks, axis=0).astype(BF16), upto)
        carry = jnp.zeros((devices, 1), F32)
        for b, (o, mark) in enumerate(zip(owners, marks)):
            part = sums[b * devices:(b + 1) * devices]
            slot = jnp.sum(mark * (part + carry), axis=0, keepdims=True) - 1.0
            pos_ref[:, b * LANES:(b + 1) * LANES] = o * cap + slot.astype(I32)
            carry = carry + part[:, LANES - 1:LANES]


def relation_step(rel, coef_t, bases_t, head_t, tail_t, owner_t, devices, cap):
    nb, nrel = coef_t.shape
    cols, triples = head_t.shape
    width = 1920
    steps = pl.cdiv(nrel, width)
    whole = lambda shape: pl.BlockSpec(shape, lambda i: (0,) * len(shape))
    outs = [((nb, triples), F32), ((cols, triples), F32), ((1, triples), F32),
            ((cols, triples), BF16), ((1, 2 * triples), I32)]
    return pl.pallas_call(
        functools.partial(relation_kernel, nrel, devices, cap),
        grid=(steps,),
        in_specs=[
            whole((1, triples)),
            pl.BlockSpec((nb, width), lambda i: (0, i)),
            whole((cols, nb)), whole((cols, triples)), whole((cols, triples)),
            whole((2, triples)),
        ],
        out_specs=[whole(s) for s, _ in outs],
        out_shape=[jax.ShapeDtypeStruct(s, d) for s, d in outs],
        scratch_shapes=[pltpu.VMEM((2 * PAD, width), BF16), pltpu.VMEM((2 * PAD, triples), F32)],
        compiler_params=params(),
        cost_estimate=cost(2 * 2 * PAD * nrel * triples, nb * nrel * 4),
        name="relation_step",
    )(rel, coef_t, bases_t, head_t, tail_t, owner_t)


def score_kernel(neg_count, negs_ref, vec_ref, head_ref, tail_ref, gate_ref, tgrad_ref, pos_ref,
                 row_ref, send_ref, probs_ref, hrel_ref, mix_ref, grads):
    group, cols, per = negs_ref.shape
    triples = head_ref.shape[1]
    vec = vec_ref[...]
    head_rel = (head_ref[...].astype(F32) * vec).astype(BF16)
    hrel_ref[...] = head_rel
    mix = jnp.zeros((cols, triples), F32)
    for first in range(0, group, 8):
        negs = jnp.concatenate([negs_ref[first + k] for k in range(8)], axis=1)
        probs = jax.nn.sigmoid(tn(negs, head_rel)).astype(BF16)
        probs_ref[first * per:(first + 8) * per] = probs
        mix = mix + nn(negs, probs)
    mix_ref[...] = mix
    tail = tail_ref[...].astype(F32)
    grads[0:cols, 0:triples] = (-gate_ref[...] * vec * tail + vec * mix / neg_count).astype(BF16)
    grads[0:cols, triples:] = tgrad_ref[...]
    for side in range(2):
        ids = row_ref[side:side + 1]
        lanes = slice(side * triples, (side + 1) * triples)
        high = ids // 64
        pair = jnp.concatenate([high, ids - high * 64], axis=0).astype(F32)
        spare = jnp.zeros((grads.shape[0] - cols - 2, triples), F32)
        grads[cols:, lanes] = jnp.concatenate([pair, spare], axis=0).astype(BF16)
    slots = 2 * LANES
    rows = send_ref.shape[1]

    @pl.loop(0, send_ref.shape[0] // 2)
    def _(b):
        part = nt(grads[...], hits(pos_ref[...], slots, b * slots)).astype(BF16)
        send_ref[2 * b] = part[0:rows, 0:LANES]
        send_ref[2 * b + 1] = part[0:rows, LANES:]


def score_step(negs, vec, head_t, tail_t, gate, tgrad, pos, rows, blocks, neg_count):
    group, cols, per = negs.shape
    triples = head_t.shape[1]
    outs = [((blocks, cols + 2, LANES), BF16), ((group * per, triples), BF16),
            ((cols, triples), BF16), ((cols, triples), F32)]
    return pl.pallas_call(
        functools.partial(score_kernel, neg_count),
        out_shape=[jax.ShapeDtypeStruct(s, d) for s, d in outs],
        scratch_shapes=[pltpu.VMEM((cols + 16, 2 * triples), BF16)],
        compiler_params=params(),
        cost_estimate=cost(2 * cols * triples * (2 * group * per + 2 * blocks * LANES), 16 << 20),
        name="score_step",
    )(negs, vec, head_t, tail_t, gate, tgrad, pos, rows)


def partial_kernel(neg_count, share, probs_ref, hrel_ref, mix_ref, head_ref, tail_ref, gate_ref,
                   picked_ref, bases_ref, rel_ref, rows_ref, parts_ref):
    group = parts_ref.shape[0]
    cols, triples = head_ref.shape
    nb = picked_ref.shape[0]
    head = head_ref[...].astype(F32)
    rel_grad = -gate_ref[...] * head * tail_ref[...].astype(F32) + head * mix_ref[...] / neg_count
    coef_rows = nn(bases_ref[...].T, rel_grad, precision=HIGHEST)
    ids = rel_ref[...]
    high = ids // 128
    pair = jnp.concatenate([high, ids - high * 128], axis=0).astype(F32)
    rows_ref[...] = jnp.concatenate([coef_rows, pair], axis=0).astype(BF16)
    base_grad = nt(picked_ref[...], rel_grad, precision=HIGHEST)
    low = base_grad - base_grad.astype(BF16).astype(F32)
    per = LANES
    for first in range(0, group, 8):
        part = nt(hrel_ref[...], probs_ref[first * per:(first + 8) * per]) / neg_count
        for k in range(8):
            parts_ref[first + k, 0:cols] = part[:, k * per:(k + 1) * per].astype(BF16)
    for k in range(group):
        first = min(k * share, cols)
        last = min(first + share, cols)
        gap = jnp.zeros((nb, 64 - max(last - first, 0)), F32)
        pieces = [base_grad[:, first:last], gap, low[:, first:last], gap]
        pieces = [p for p in pieces if p.shape[1] > 0]
        parts_ref[k, cols:] = jnp.concatenate(pieces, axis=1).astype(BF16)


def partial_step(probs, hrel, mix, head_t, tail_t, gate, picked, bases_t, rel, group, share,
                 neg_count):
    cols, triples = head_t.shape
    nb = picked.shape[0]
    outs = [((nb + 2, triples), BF16), ((group, cols + nb, LANES), BF16)]
    return pl.pallas_call(
        functools.partial(partial_kernel, neg_count, share),
        out_shape=[jax.ShapeDtypeStruct(s, d) for s, d in outs],
        compiler_params=params(),
        cost_estimate=cost(1, 1),
        name="partial_step",
    )(probs, hrel, mix, head_t, tail_t, gate, picked, bases_t, rel)


def gather_coef_kernel(span, share, me_ref, *refs):
    row_refs, parts_ref, out_ref = refs[:-2], refs[-2], refs[-1]
    step = pl.program_id(0)
    nb, width = out_ref.shape[1], out_ref.shape[2]
    first = step * width
    total = jnp.zeros((nb, width), F32)
    for ref in row_refs:
        for s in range(ref.shape[0]):
            ids = (ref[s, nb:nb + 1].astype(F32) * 128.0 + ref[s, nb + 1:nb + 2].astype(F32))
            ids = ids.astype(I32) - me_ref[0] * span
            ids = jnp.where((ids >= 0) & (ids < span), ids, -1)
            total = total + nt(ref[s, 0:nb], hits(ids, width, first))
    out_ref[0] = total

    @pl.when(step == span // width)
    def _():
        both = jnp.sum(parts_ref[:, parts_ref.shape[1] - nb:].astype(F32), axis=0)
        at = span % width
        out_ref[0, :, at:at + share] = both[:, 0:share] + both[:, 64:64 + share]


def gather_coef(me, row_sets, parts, span, share, width, quarters):
    nb = row_sets[0].shape[1] - 2
    whole = lambda shape: pl.BlockSpec(shape, lambda i, me: (0,) * len(shape))
    return pl.pallas_call(
        functools.partial(gather_coef_kernel, span, share),
        grid_spec=pltpu.PrefetchScalarGridSpec(
            num_scalar_prefetch=1,
            grid=(quarters,),
            in_specs=[whole(r.shape) for r in row_sets] + [whole(parts.shape)],
            out_specs=pl.BlockSpec((1, nb, width), lambda i, me: (i, 0, 0)),
        ),
        out_shape=jax.ShapeDtypeStruct((quarters, nb, width), F32),
        compiler_params=params(),
        cost_estimate=cost(1, 1),
        name="gather_coef",
    )(me, *row_sets, parts)


def spread_kernel(span, share, where_ref, which_ref, a_ref, b_ref, coef_ref, base_ref, pieces):
    step = pl.program_id(0)
    steps = pl.num_programs(0)
    quarters, width = a_ref.shape[1], a_ref.shape[3]
    cols = base_ref.shape[1]

    def put(ref):
        for q in range(quarters):
            first = q * width
            if first < span:
                last = min(first + width, span)
                coef_ref[:, first:last] = ref[0, q, :, 0:last - first].astype(F32)
        at = span % width
        piece = ref[0, span // width, :, at:at + LANES].astype(F32)
        spare = jnp.zeros((pieces.shape[1] - piece.shape[0], LANES), F32)
        pieces[step] = jnp.concatenate([piece, spare], axis=0)

    @pl.when(which_ref[step] == 0)
    def _():
        put(a_ref)

    @pl.when(which_ref[step] != 0)
    def _():
        put(b_ref)

    @pl.when(step == steps - 1)
    def _():
        count = pieces.shape[0]
        row = jnp.concatenate([pieces[k][:, 0:share] for k in range(count)], axis=1)
        base_ref[...] = row[0:base_ref.shape[0], 0:cols]


def spread(where, which, a, b, span, share, nrel, cols):
    group = where.shape[0]
    _, quarters, nb, width = a.shape
    pick = lambda i, where, which: (where[i], 0, 0, 0)
    return pl.pallas_call(
        functools.partial(spread_kernel, span, share),
        grid_spec=pltpu.PrefetchScalarGridSpec(
            num_scalar_prefetch=2,
            grid=(group,),
            in_specs=[pl.BlockSpec((1, quarters, nb, width), pick)] * 2,
            out_specs=[
                pl.BlockSpec((nb, span), lambda i, where, which: (0, i)),
                pl.BlockSpec((nb, cols), lambda i, where, which: (0, 0)),
            ],
            scratch_shapes=[pltpu.VMEM((group, PAD, LANES), F32)],
        ),
        out_shape=[jax.ShapeDtypeStruct((nb, nrel), F32), jax.ShapeDtypeStruct((nb, cols), F32)],
        compiler_params=params(),
        cost_estimate=cost(1, 1),
        name="spread",
    )(where, which, a, b)


def add_rows_kernel(recv_ref, parts_ref, neg_ref, out_ref, grads, ids, negs):
    step = pl.program_id(0)
    cols, width = out_ref.shape
    sources = recv_ref.shape[0]

    @pl.when(step == 0)
    def _():
        for s in range(sources):
            lanes = slice(s * LANES, (s + 1) * LANES)
            grads[:, lanes] = recv_ref[s, 0:cols]
            pair = recv_ref[s, cols:cols + 2].astype(F32)
            ids[:, lanes] = (pair[0:1] * 64.0 + pair[1:2]).astype(I32)
        total = parts_ref[0, 0:cols].astype(F32)
        for k in range(1, parts_ref.shape[0]):
            total = total + parts_ref[k, 0:cols].astype(F32)
        top = total.astype(BF16)
        negs[:, 0:LANES] = top
        negs[:, LANES:] = (total - top.astype(F32)).astype(BF16)

    first = step * width
    mine = hits(neg_ref[...], width, first)
    out_ref[...] = nt(grads[...], hits(ids[...], width, first)) + nt(
        negs[...], jnp.concatenate([mine, mine], axis=1))


def add_rows(recv, parts, neg_ids, cols, ent):
    sources = recv.shape[0]
    width = 512
    whole = lambda shape: pl.BlockSpec(shape, lambda i: (0,) * len(shape))
    return pl.pallas_call(
        add_rows_kernel,
        grid=(ent // width,),
        in_specs=[whole(recv.shape), whole(parts.shape), whole(neg_ids.shape)],
        out_specs=pl.BlockSpec((cols, width), lambda i: (0, i)),
        out_shape=jax.ShapeDtypeStruct((cols, ent), F32),
        scratch_shapes=[pltpu.VMEM((cols, sources * LANES), BF16),
                        pltpu.VMEM((1, sources * LANES), I32),
                        pltpu.VMEM((cols, 2 * LANES), BF16)],
        compiler_params=params(),
        cost_estimate=cost(1, 1),
        name="add_rows",
    )(recv, parts, neg_ids)


def from_group(block, group):
    numbers = jnp.arange(group, dtype=I32)
    if group != 8:
        everything = lax.all_gather(block, "dev", axis=0)
        return everything, everything, numbers, jnp.zeros_like(numbers)
    own = [block] + [
        lax.ppermute(block, "dev", [(i, i ^ far) for i in range(group)]) for far in (2, 4, 6)
    ]
    own = jnp.stack(own)
    sibling = lax.ppermute(own, "dev", [(i, i ^ 1) for i in range(group)])
    offset = numbers ^ lax.axis_index("dev").astype(I32)
    return own, sibling, offset // 2, offset % 2


def per_device(head_emb, tail_emb, relation, owners, owner_rows, entities, neg_rows, coef, bases):
    triples, cols = head_emb.shape
    group = lax.axis_size("dev")
    layers = lax.axis_size("grp")
    devices = layers * group
    neg_count = neg_rows.shape[1] * group
    ent_local = entities.shape[0]
    nrel, nb = coef.shape
    cap = 4 * triples // devices
    blocks = devices * cap // LANES
    share = pl.cdiv(cols, group)
    span = pl.cdiv(pl.cdiv(nrel, group), LANES) * LANES
    quarter = pl.cdiv(span + LANES, layers * LANES) * LANES

    head_t, tail_t, owner_t, row_t = head_emb.T, tail_emb.T, owners.T, owner_rows.T
    coef_t, bases_t = coef.T, bases.T
    rel = relation.reshape(1, triples)

    sent_negs = pick_negs(neg_rows, entities.T, group)
    negs = lax.all_to_all(sent_negs, "dev", 0, 0, tiled=True)
    picked, vec, gate, tgrad, pos = relation_step(
        rel, coef_t, bases_t, head_t, tail_t, owner_t, devices, cap)
    send, probs, hrel, mix = score_step(
        negs, vec, head_t, tail_t, gate, tgrad, pos, row_t, blocks, neg_count)
    per_block = LANES // cap
    if per_block > 1:
        send = send.reshape(blocks, cols + 2, per_block, cap).transpose(0, 2, 1, 3)
        send = send.reshape(devices, cols + 2, cap)
    recv = lax.all_to_all(send, ("grp", "dev"), 0, 0, tiled=True)
    if per_block > 1:
        recv = recv.reshape(blocks, per_block, cols + 2, cap).transpose(0, 2, 1, 3)
        recv = recv.reshape(blocks, cols + 2, LANES)

    rows, parts = partial_step(
        probs, hrel, mix, head_t, tail_t, gate, picked, bases_t, rel, group, share, neg_count)
    own_rows, sibling_rows, _, _ = from_group(rows, group)
    parts = lax.all_to_all(parts, "dev", 0, 0, tiled=True)
    me = lax.axis_index("dev").astype(I32).reshape(1)
    row_sets = [own_rows, sibling_rows] if group == 8 else [own_rows]
    columns = gather_coef(me, row_sets, parts, span, share, quarter, layers)
    columns = lax.all_to_all(columns, "grp", 0, 0, tiled=True)
    columns = jnp.sum(columns, axis=0).astype(BF16)
    columns = lax.all_gather(columns, "grp", axis=0)
    a, b, where, which = from_group(columns, group)
    coef_grad, bases_grad = spread(where, which, a, b, span, share, nrel, cols)

    ent_grad = add_rows(recv, parts, neg_rows, cols, ent_local)
    return ent_grad.T, coef_grad.T, bases_grad


def solution(mesh):
    return jax.shard_map(
        per_device,
        mesh=mesh,
        in_specs=(
            P(("grp", "dev"), None),
            P(("grp", "dev"), None),
            P(("grp", "dev")),
            P(("grp", "dev"), None),
            P(("grp", "dev"), None),
            P(("grp", "dev"), None),
            P(None, ("grp", "dev")),
            P(),
            P(),
        ),
        out_specs=(P(("grp", "dev"), None), P(), P()),
        check_vma=False,
    )
```

```python
import functools
import math

import jax
import jax.numpy as jnp
from jax import lax
from jax.experimental import pallas as pl
from jax.experimental.pallas import tpu as pltpu
from jax.sharding import PartitionSpec as P

F32, BF16, I32 = jnp.float32, jnp.bfloat16, jnp.int32
LANES = 128
PAD = 112
VMEM_BYTES = 56 * 1024 * 1024


def nt(a, b, **kw):
    return lax.dot_general(a, b, (((1,), (1,)), ((), ())), preferred_element_type=F32, **kw)


def tn(a, b, **kw):
    return lax.dot_general(a, b, (((0,), (0,)), ((), ())), preferred_element_type=F32, **kw)


def nn(a, b, **kw):
    return lax.dot_general(a, b, (((1,), (0,)), ((), ())), preferred_element_type=F32, **kw)


def split(x):
    top = x.astype(BF16)
    return top, (x - top.astype(F32)).astype(BF16)


def padded(x):
    more = -x.shape[0] % 16
    return jnp.concatenate([x, jnp.zeros((more, x.shape[1]), x.dtype)], axis=0) if more else x


def precise(product, a, b):
    rows = a.shape[0]
    a = padded(a)
    tall = a.shape[0]
    a_top, a_low = split(a)
    b_top, b_low = split(b)
    both = product(jnp.concatenate([a_top, a_low], axis=0), b_top)
    return (both[0:tall] + both[tall:] + product(a_top, b_low))[0:rows]


def params():
    return pltpu.CompilerParams(vmem_limit_bytes=VMEM_BYTES)


def cost(flops, nbytes):
    return pl.CostEstimate(flops=flops, bytes_accessed=nbytes, transcendentals=0)


def hits(ids, rows, first):
    row = lax.broadcasted_iota(I32, (rows, ids.shape[1]), 0)
    return jnp.where(row == ids - first, 1.0, 0.0).astype(BF16)


def pick_negs_kernel(ids_ref, ent_ref, out_ref, acc_ref):
    step = pl.program_id(0)
    width = ent_ref.shape[1]
    part = nn(ent_ref[...], hits(ids_ref[...], width, step * width))

    @pl.when(step == 0)
    def _():
        acc_ref[...] = part

    @pl.when(step > 0)
    def _():
        acc_ref[...] += part

    @pl.when(step == pl.num_programs(0) - 1)
    def _():
        rows = acc_ref[...].astype(BF16)
        for k in range(out_ref.shape[0]):
            out_ref[k] = rows


def pick_negs(ids, ent_t, group):
    cols, ent = ent_t.shape
    width = 1024
    return pl.pallas_call(
        pick_negs_kernel,
        grid=(ent // width,),
        in_specs=[
            pl.BlockSpec((1, ids.shape[1]), lambda i: (0, 0)),
            pl.BlockSpec((cols, width), lambda i: (0, i)),
        ],
        out_specs=pl.BlockSpec((group, cols, ids.shape[1]), lambda i: (0, 0, 0)),
        out_shape=jax.ShapeDtypeStruct((group, cols, ids.shape[1]), BF16),
        scratch_shapes=[pltpu.VMEM((cols, ids.shape[1]), F32)],
        compiler_params=params(),
        cost_estimate=cost(2 * cols * ent * 128, cols * ent * 2),
        name="pick_negs",
    )(ids, ent_t)


def up_to_here():
    rows = lax.broadcasted_iota(I32, (LANES, LANES), 0)
    cols = lax.broadcasted_iota(I32, (LANES, LANES), 1)
    return jnp.where(rows <= cols, 1.0, 0.0).astype(BF16)


def relation_kernel(nrel, devices, plan, rel_ref, coef_ref, bases_ref, head_ref, tail_ref,
                    picked_ref, vec_ref, gate_ref, tgrad_ref, place_ref, halves, acc):
    step = pl.program_id(0)
    width = coef_ref.shape[1]
    nb = coef_ref.shape[0]
    lane = lax.broadcasted_iota(I32, (nb, width), 1) + step * width
    block = jnp.where(lane < nrel, coef_ref[...], 0.0)
    low = block - block.astype(BF16).astype(F32)
    tall = acc.shape[0] // 2
    spare = [jnp.zeros((tall - nb, width), F32)] * (tall > nb)
    halves[...] = jnp.concatenate([block, *spare, low, *spare], axis=0).astype(BF16)

    @pl.when(step == 0)
    def _():
        acc[...] = jnp.zeros_like(acc)

    acc[...] += nn(halves[...], hits(rel_ref[...], width, step * width))

    @pl.when(step == pl.num_programs(0) - 1)
    def _():
        picked = acc[0:nb] + acc[tall:tall + nb]
        picked_ref[...] = picked
        vec = precise(nn, bases_ref[...], picked)
        vec_ref[...] = vec
        head = head_ref[...].astype(F32)
        head_vec = head * vec
        score = jnp.sum(head_vec * tail_ref[...].astype(F32), axis=0, keepdims=True)
        gate = jax.nn.sigmoid(-score)
        gate_ref[...] = gate
        tgrad_ref[...] = (-gate * head * vec).astype(BF16)
        triples = rel_ref.shape[1]
        upto = up_to_here()
        number = lax.broadcasted_iota(I32, (devices, LANES), 0)
        span, slots, room = plan
        rel = rel_ref[...]
        later = lax.broadcasted_iota(I32, (LANES, triples), 1)
        row = lax.broadcasted_iota(I32, (LANES, triples), 0)
        seen = jnp.zeros((1, triples), F32)
        same = []
        for b in range(triples // LANES):
            down = jnp.broadcast_to(
                rel[:, b * LANES:(b + 1) * LANES].astype(F32), (LANES, LANES)).T[:, 0:1]
            equal = jnp.where(down.astype(I32) == rel, 1.0, 0.0)
            same.append(equal.astype(BF16))
            before = jnp.where(row + b * LANES < later, equal, 0.0)
            seen = seen + jnp.sum(before, axis=0, keepdims=True)
        first = jnp.where(seen == 0.0, 1.0, 0.0)
        summer = rel // span
        marks = []
        for b in range(triples // LANES):
            lanes = slice(b * LANES, (b + 1) * LANES)
            marks.append(jnp.where(number == summer[:, lanes], first[:, lanes], 0.0))
        sums = nn(jnp.concatenate(marks, axis=0).astype(BF16), upto)
        carry = jnp.zeros((devices, 1), F32)
        lead = []
        for b, mark in enumerate(marks):
            part = sums[b * devices:(b + 1) * devices]
            lead.append(jnp.sum(mark * (part + carry - 1.0), axis=0, keepdims=True))
            carry = carry + part[:, LANES - 1:LANES]
        lead = jnp.minimum(jnp.concatenate(lead, axis=1), 255.0)
        lead = jnp.broadcast_to(lead, (16, triples)).astype(BF16)
        slot = nn(lead, jnp.concatenate(same, axis=0))[0:1].astype(I32)
        fits = slot < room
        place_ref[0:1] = jnp.where(fits, summer * slots + slot, -1)
        place_ref[1:2] = jnp.where(seen == 0.0, rel - summer * span, -1)
        over = jnp.max(jnp.where(fits, 0, 1), axis=1, keepdims=True)
        place_ref[2:3] = jnp.broadcast_to(over, (1, triples))


def relation_step(rel, coef_t, bases_t, head_t, tail_t, devices, plan):
    nb, nrel = coef_t.shape
    cols, triples = head_t.shape
    width = 1920
    steps = pl.cdiv(nrel, width)
    tall = pl.cdiv(nb, 8) * 8
    whole = lambda shape: pl.BlockSpec(shape, lambda i: (0,) * len(shape))
    outs = [((nb, triples), F32), ((cols, triples), F32), ((1, triples), F32),
            ((cols, triples), BF16), ((3, triples), I32)]
    return pl.pallas_call(
        functools.partial(relation_kernel, nrel, devices, plan),
        grid=(steps,),
        in_specs=[
            whole((1, triples)),
            pl.BlockSpec((nb, width), lambda i: (0, i)),
            whole((cols, nb)), whole((cols, triples)), whole((cols, triples)),
        ],
        out_specs=[whole(s) for s, _ in outs],
        out_shape=[jax.ShapeDtypeStruct(s, d) for s, d in outs],
        scratch_shapes=[pltpu.VMEM((2 * tall, width), BF16), pltpu.VMEM((2 * tall, triples), F32)],
        compiler_params=params(),
        cost_estimate=cost(2 * 2 * PAD * nrel * triples, nb * nrel * 4),
        name="relation_step",
    )(rel, coef_t, bases_t, head_t, tail_t)


def score_kernel(neg_count, negs_ref, vec_ref, head_ref, tail_ref, gate_ref, tgrad_ref, row_ref,
                 bases_ref, picked_ref, grads_ref, rows_ref, base_ref, probs_ref, hrel_ref):
    group, cols, per = negs_ref.shape
    triples = head_ref.shape[1]
    vec = vec_ref[...]
    head = head_ref[...].astype(F32)
    head_rel = (head * vec).astype(BF16)
    hrel_ref[...] = head_rel
    mix = jnp.zeros((cols, triples), F32)
    for first in range(0, group, 8):
        negs = jnp.concatenate([negs_ref[first + k] for k in range(8)], axis=1)
        probs = jax.nn.sigmoid(tn(negs, head_rel)).astype(BF16)
        probs_ref[first * per:(first + 8) * per] = probs
        mix = mix + nn(negs, probs)
    tail = tail_ref[...].astype(F32)
    gate = gate_ref[...]
    rel_grad = -gate * head * tail + head * mix / neg_count
    rows_ref[...] = precise(nn, bases_ref[...].T, rel_grad)
    base_ref[...] = precise(nt, picked_ref[...], rel_grad)
    grads_ref[0:cols, 0:triples] = (-gate * vec * tail + vec * mix / neg_count).astype(BF16)
    grads_ref[0:cols, triples:] = tgrad_ref[...]
    for side in range(2):
        ids = row_ref[side:side + 1]
        lanes = slice(side * triples, (side + 1) * triples)
        high = ids // 64
        pair = jnp.concatenate([high, ids - high * 64], axis=0).astype(F32)
        more = grads_ref.shape[0] - cols - 2
        if more:
            pair = jnp.concatenate([pair, jnp.zeros((more, triples), F32)], axis=0)
        grads_ref[cols:, lanes] = pair.astype(BF16)


def score_step(negs, vec, head_t, tail_t, gate, tgrad, rows, bases_t, picked, tall, neg_count):
    group, cols, per = negs.shape
    triples = head_t.shape[1]
    nb = bases_t.shape[1]
    outs = [((tall, 2 * triples), BF16), ((nb, triples), F32), ((nb, cols), F32),
            ((group * per, triples), BF16), ((cols, triples), BF16)]
    return pl.pallas_call(
        functools.partial(score_kernel, neg_count),
        out_shape=[jax.ShapeDtypeStruct(s, d) for s, d in outs],
        compiler_params=params(),
        cost_estimate=cost(2 * cols * triples * 2 * group * per, 16 << 20),
        name="score_step",
    )(negs, vec, head_t, tail_t, gate, tgrad, rows, bases_t, picked)


def band(rows, slots):
    bands = LANES // slots
    return rows if bands == 1 else pl.cdiv(pl.cdiv(rows, bands), 16) * 16


def order_kernel(devices, slots, grads_ref, owner_ref, send_ref, pos):
    owners, high, _ = send_ref.shape
    bands = LANES // slots
    step = pl.program_id(0)

    @pl.when(step == 0)
    def _():
        owner = owner_ref[...]
        triples = owner.shape[1]
        number = lax.broadcasted_iota(I32, (devices, LANES), 0)
        parts, marks = [], []
        for side in range(2):
            for b in range(triples // LANES):
                part = owner[side:side + 1, b * LANES:(b + 1) * LANES]
                parts.append(part)
                marks.append(jnp.where(number == part, 1.0, 0.0))
        sums = nn(jnp.concatenate(marks, axis=0).astype(BF16), up_to_here())
        carry = jnp.zeros((devices, 1), F32)
        for b, (part, mark) in enumerate(zip(parts, marks)):
            here = sums[b * devices:(b + 1) * devices]
            slot = jnp.sum(mark * (here + carry), axis=0, keepdims=True) - 1.0
            pos[:, b * LANES:(b + 1) * LANES] = part * slots + slot.astype(I32)
            carry = carry + here[:, LANES - 1:LANES]

    part = nt(grads_ref[...], hits(pos[...], owners * slots, step * owners * slots))
    part = part.astype(BF16)
    for o in range(owners):
        at = o * slots
        block = [part[b * high:(b + 1) * high, at:at + slots] for b in range(bands)]
        send_ref[o] = jnp.concatenate(block, axis=1)


def order_slots(grads, owner_t, devices, slots, rows):
    owners = 512 // slots
    high = band(rows, slots)
    whole = lambda shape: pl.BlockSpec(shape, lambda i: (0,) * len(shape))
    return pl.pallas_call(
        functools.partial(order_kernel, devices, slots),
        grid=(devices // owners,),
        in_specs=[whole(grads.shape), whole(owner_t.shape)],
        out_specs=pl.BlockSpec((owners, high, LANES), lambda i: (i, 0, 0)),
        out_shape=jax.ShapeDtypeStruct((devices, high, LANES), BF16),
        scratch_shapes=[pltpu.VMEM((1, grads.shape[1]), I32)],
        compiler_params=params(),
        cost_estimate=cost(rows * grads.shape[1] * devices * slots * 2, 4 << 20),
        name="order_slots",
    )(grads, owner_t)


def partial_kernel(neg_count, me_ref, probs_ref, hrel_ref, parts_ref, block):
    half, per = parts_ref.shape[1], parts_ref.shape[3]
    for first in range(0, 2 * half, 8):
        part = nt(hrel_ref[...], probs_ref[first * per:(first + 8) * per]) / neg_count
        block[...] = part
        for k in range(8):
            lane = pl.multiple_of((k ^ me_ref[0]) * per, per)
            parts_ref[k % 2, (first + k) // 2] = block[:, pl.ds(lane, per)].astype(BF16)


def partial_step(me, probs, hrel, group, neg_count):
    cols = hrel.shape[0]
    whole = lambda shape: pl.BlockSpec(shape, lambda i, me: (0,) * len(shape))
    shape = (2, group // 2, cols, LANES)
    return pl.pallas_call(
        functools.partial(partial_kernel, neg_count),
        grid_spec=pltpu.PrefetchScalarGridSpec(
            num_scalar_prefetch=1,
            grid=(1,),
            in_specs=[whole(probs.shape), whole(hrel.shape)],
            out_specs=whole(shape),
            scratch_shapes=[pltpu.VMEM((cols, 8 * LANES), F32)],
        ),
        out_shape=jax.ShapeDtypeStruct(shape, BF16),
        compiler_params=params(),
        cost_estimate=cost(1, 1),
        name="partial_step",
    )(me, probs, hrel)


def coef_order_kernel(plan, share, rows_ref, base_ref, place_ref, send_ref):
    span, slots, room = plan
    devices, high, _ = send_ref.shape
    nb, triples = rows_ref.shape
    cols = base_ref.shape[1]
    lanes = devices * slots

    def halves(block):
        spare = jnp.zeros((PAD - block.shape[0], block.shape[1]), F32)
        block = jnp.concatenate([block, spare], axis=0)
        top = block.astype(BF16)
        return jnp.concatenate([top, (block - top.astype(F32)).astype(BF16)], axis=0)

    local = place_ref[1:2]
    lead = local >= 0
    high_id = local // 64
    pair = jnp.concatenate([high_id, local - high_id * 64], axis=0)
    pair = jnp.where(lead, pair, 0).astype(F32)
    left = halves(jnp.concatenate([rows_ref[...], pair], axis=0))
    both = nt(left, hits(place_ref[0:1], lanes, 0))
    column = lax.broadcasted_iota(I32, (1, cols), 1)
    owner = column // share
    spots = owner * slots + room + column - owner * share
    both = both + nt(halves(base_ref[...]), hits(spots, lanes, 0))
    both = both[0:PAD] + both[PAD:]
    row = lax.broadcasted_iota(I32, (PAD, lanes), 0)
    both = jnp.where(row == nb + 2, place_ref[2:3, 0:1].astype(F32), both)
    bands = LANES // slots
    if bands * high > PAD:
        both = jnp.concatenate([both, jnp.zeros((bands * high - PAD, lanes), F32)], axis=0)
    for o in range(devices):
        block = [both[b * high:(b + 1) * high, o * slots:(o + 1) * slots] for b in range(bands)]
        send_ref[o] = jnp.concatenate(block, axis=1).astype(BF16)


def coef_order(rows, base, place, devices, plan, share):
    high = pl.cdiv(PAD * plan[1], 8 * LANES) * 8
    return pl.pallas_call(
        functools.partial(coef_order_kernel, plan, share),
        out_shape=jax.ShapeDtypeStruct((devices, high, LANES), BF16),
        compiler_params=params(),
        cost_estimate=cost(1, 1),
        name="coef_order",
    )(rows, base, place)


def coef_sum_kernel(nb, plan, recv_ref, out_ref, flag_ref, left):
    span, slots, room = plan
    sources, high, _ = recv_ref.shape
    bands = LANES // slots
    for s in range(0, sources, bands):
        lanes = slice(s * slots, (s + bands) * slots)
        tall = []
        for b in range(bands):
            block = [recv_ref[s + k, :, b * slots:(b + 1) * slots] for k in range(bands)]
            tall.append(jnp.concatenate(block, axis=1).astype(F32))
        left[:, lanes] = jnp.concatenate(tall, axis=0)[0:PAD].astype(BF16)
    extra = left[PAD - 16:PAD].astype(F32)
    at = nb - (PAD - 16)
    ids = (extra[at:at + 1] * 64.0 + extra[at + 1:at + 2]).astype(I32)
    lane = lax.broadcasted_iota(I32, ids.shape, 1)
    lane = lane - lane // slots * slots
    ids = jnp.where(lane < room, ids, span + lane - room)
    total = nt(left[0:PAD], hits(ids, out_ref.shape[1], 0))
    out_ref[...] = total[0:nb].astype(BF16)
    over = jnp.max(extra[at + 2:at + 3], axis=1, keepdims=True)
    flag_ref[...] = jnp.broadcast_to(over, flag_ref.shape).astype(I32)


def coef_sum(recv, nb, plan, width):
    sources = recv.shape[0]
    slots = plan[1]
    return pl.pallas_call(
        functools.partial(coef_sum_kernel, nb, plan),
        out_shape=[jax.ShapeDtypeStruct((nb, width), BF16), jax.ShapeDtypeStruct((1, LANES), I32)],
        scratch_shapes=[pltpu.VMEM((PAD, sources * slots), BF16)],
        compiler_params=params(),
        cost_estimate=cost(1, 1),
        name="coef_sum",
    )(recv)


def spread_kernel(span, share, place_ref, *refs):
    sets, (coef_ref, base_ref, pieces, strips) = refs[:-4], refs[-4:]
    step = pl.program_id(0)
    group, layers, nb, _ = pieces.shape

    @pl.when(step == 0)
    def _():
        number = 0
        for ref in sets:
            for s in range(ref.shape[0]):
                pieces[number ^ place_ref[0]] = ref[s]
                number += 1

    slab = lax.rem(place_ref[1] - step + layers, layers)
    row = [pieces[k, slab].astype(F32) for k in range(group)]
    coef_ref[...] = jnp.concatenate([r[:, 0:span] for r in row], axis=1)
    strip = jnp.concatenate([r[:, span:span + share] for r in row], axis=1)
    strips[step] = jnp.concatenate([strip, jnp.zeros((PAD - nb, strip.shape[1]), F32)], axis=0)

    @pl.when(step == layers - 1)
    def _():
        whole = jnp.concatenate([strips[g] for g in range(layers)], axis=1)
        base_ref[...] = whole[0:nb, 0:base_ref.shape[0]].T


def spread(me, layer, sets, span, share, nrel, cols):
    group = sum(s.shape[0] for s in sets)
    _, layers, nb, width = sets[0].shape
    whole = lambda shape: pl.BlockSpec(shape, lambda i, place: (0,) * len(shape))
    return pl.pallas_call(
        functools.partial(spread_kernel, span, share),
        grid_spec=pltpu.PrefetchScalarGridSpec(
            num_scalar_prefetch=1,
            grid=(layers,),
            in_specs=[whole(s.shape) for s in sets],
            out_specs=[
                pl.BlockSpec((nb, group * span), lambda i, place: (0, i)),
                whole((cols, nb)),
            ],
            scratch_shapes=[pltpu.VMEM((group, layers, nb, width), BF16),
                            pltpu.VMEM((layers, PAD, group * share), F32)],
        ),
        out_shape=[jax.ShapeDtypeStruct((nb, nrel), F32), jax.ShapeDtypeStruct((cols, nb), F32)],
        compiler_params=params(),
        cost_estimate=cost(1, 1),
        name="spread",
    )(jnp.concatenate([me, layer]), *sets)


def add_rows_kernel(slots, recv_ref, neg_ref, *refs):
    part_refs, (out_ref, grads, ids, sems) = refs[:-4], refs[-4:]
    step = pl.program_id(0)
    cols, width = out_ref.shape
    sources, high, _ = recv_ref.shape
    bands = LANES // slots
    lanes = sources * slots

    @pl.when(step == 0)
    def _():
        copies = []
        if bands == 1:
            for s in range(sources):
                to = grads.at[:, s * slots:(s + 1) * slots]
                copies.append(pltpu.make_async_copy(recv_ref.at[s], to, sems.at[s]))
        else:
            for s in range(0, sources, bands):
                at = slice(s * slots, (s + bands) * slots)
                for b in range(bands):
                    block = [recv_ref[s + k, :, b * slots:(b + 1) * slots] for k in range(bands)]
                    grads[b * high:(b + 1) * high, at] = jnp.concatenate(block, axis=1)
        for copy in copies:
            copy.start()
        total = jnp.zeros((cols, LANES), F32)
        for ref in part_refs:
            for k in range(ref.shape[0]):
                total = total + ref[k].astype(F32)
        top, low = split(total)
        grads[0:cols, lanes:lanes + LANES] = top
        grads[0:cols, lanes + LANES:] = low
        ids[:, lanes:lanes + LANES] = neg_ref[...]
        ids[:, lanes + LANES:] = neg_ref[...]
        for copy in copies:
            copy.wait()
        pair = grads[cols:cols + 2, 0:lanes].astype(F32)
        ids[:, 0:lanes] = (pair[0:1] * 64.0 + pair[1:2]).astype(I32)

    out_ref[...] = nt(grads[0:cols], hits(ids[...], width, step * width))


def add_rows(recv, slots, cols, ent, neg_ids, part_sets):
    sources, high, _ = recv.shape
    bands = LANES // slots
    width = 1024
    lanes = sources * slots + 2 * LANES
    whole = lambda shape: pl.BlockSpec(shape, lambda i: (0,) * len(shape))
    there = pl.BlockSpec(memory_space=pltpu.HBM) if bands == 1 else whole(recv.shape)
    return pl.pallas_call(
        functools.partial(add_rows_kernel, slots),
        grid=(ent // width,),
        in_specs=[there] + [whole(r.shape) for r in (neg_ids, *part_sets)],
        out_specs=pl.BlockSpec((cols, width), lambda i: (0, i)),
        out_shape=jax.ShapeDtypeStruct((cols, ent), F32),
        scratch_shapes=[pltpu.VMEM((bands * high, lanes), BF16),
                        pltpu.VMEM((1, lanes), I32),
                        pltpu.SemaphoreType.DMA((sources,))],
        compiler_params=params(),
        cost_estimate=cost(1, 1),
        name="add_rows",
    )(recv, neg_ids, *part_sets)


def from_group(block, group):
    block = block[None]
    if group != 8:
        return [lax.all_gather(block, "dev", axis=0, tiled=True)]
    swap = lambda x, far: lax.ppermute(x, "dev", [(i, i ^ far) for i in range(group)])
    blocks = {0: block, 2: swap(block, 2), 4: swap(block, 4), 6: swap(block, 6)}
    for far in (0, 2, 4, 6):
        blocks[far + 1] = swap(blocks[far], 1)
    return [blocks[t] for t in range(group)]


def sum_here(parts, group):
    if group != 8:
        parts = parts.swapaxes(0, 1).reshape((group,) + parts.shape[2:])
        return [lax.all_to_all(parts, "dev", 0, 0, tiled=True)]
    swap = lambda x, far: lax.ppermute(x, "dev", [(i, i ^ far) for i in range(group)])
    pairs = parts[0].astype(F32) + swap(parts[1], 1).astype(F32)
    pairs = pairs.astype(BF16)
    return [pairs[0:1]] + [swap(pairs[n:n + 1], 2 * n) for n in (1, 2, 3)]


def shift_layers(block, far, layers):
    return lax.ppermute(block, "grp", [(i, (i + far) % layers) for i in range(layers)])


def everywhere(values):
    for axis in ("dev", "grp"):
        count = lax.axis_size(axis)
        ring = [(i, (i + 1) % count) for i in range(count)]

        def turn(_, state):
            near = tuple(lax.ppermute(v, axis, ring) for v in state[0])
            return near, tuple(t + n for t, n in zip(state[1], near))

        values = lax.fori_loop(0, count - 1, turn, (values, values))[1]
    return values


def per_device(head_emb, tail_emb, relation, owners, owner_rows, entities, neg_rows, coef, bases):
    triples, cols = head_emb.shape
    group = lax.axis_size("dev")
    layers = lax.axis_size("grp")
    devices = layers * group
    neg_count = neg_rows.shape[1] * group
    ent_local = entities.shape[0]
    nrel, nb = coef.shape
    cap = 4 * triples // devices
    tall = LANES // cap * band(cols + 2, cap)
    share = pl.cdiv(cols, devices)
    step = LANES // math.gcd(group, LANES)
    span = pl.cdiv(pl.cdiv(nrel, devices), step) * step
    slots = 2 * triples // devices
    plan = (span, slots, slots - share)
    width = pl.cdiv(span + share, LANES) * LANES

    head_t, tail_t, owner_t, row_t = head_emb.T, tail_emb.T, owners.T, owner_rows.T
    coef_t, bases_t = coef.T, bases.T
    rel = relation.reshape(1, triples)

    sent_negs = pick_negs(neg_rows, entities.T, group)
    negs = lax.all_to_all(sent_negs, "dev", 0, 0, tiled=True)
    picked, vec, gate, tgrad, place = relation_step(
        rel, coef_t, bases_t, head_t, tail_t, devices, plan)
    grads, rows, base, probs, hrel = score_step(
        negs, vec, head_t, tail_t, gate, tgrad, row_t, bases_t, picked, tall, neg_count)
    coef_send = coef_order(rows, base, place, devices, plan, share)
    coef_recv = lax.all_to_all(coef_send, ("grp", "dev"), 0, 0, tiled=True)
    send = order_slots(grads, owner_t, devices, cap, cols + 2)
    send, coef_recv = lax.optimization_barrier((send, coef_recv))
    piece, flag = coef_sum(coef_recv, nb, plan, width)
    slabs = [piece] + [shift_layers(piece, far, layers) for far in range(1, layers)]
    send, slabs = lax.optimization_barrier((send, slabs))
    recv = lax.all_to_all(send, ("grp", "dev"), 0, 0, tiled=True)

    me = lax.axis_index("dev").astype(I32).reshape(1)
    layer = lax.axis_index("grp").astype(I32).reshape(1)
    at = me if group == 8 else jnp.zeros((1,), I32)
    pieces = from_group(jnp.stack(slabs), group)

    def packed():
        return tuple(spread(at, layer, pieces, span, share, nrel, cols))

    def dense():
        return everywhere((jnp.zeros((nb, nrel), F32).at[:, relation].add(rows), base.T))

    parts = sum_here(partial_step(at, probs, hrel, group, neg_count), group)
    parts, pieces = lax.optimization_barrier((parts, pieces))
    coef_grad, bases_grad = lax.cond(flag[0, 0] == 0, packed, dense)
    ent_grad = add_rows(recv, cap, cols, ent_local, neg_rows, parts)
    return ent_grad.T, coef_grad.T, bases_grad.T


def solution(mesh):
    return jax.shard_map(
        per_device,
        mesh=mesh,
        in_specs=(
            P(("grp", "dev"), None),
            P(("grp", "dev"), None),
            P(("grp", "dev")),
            P(("grp", "dev"), None),
            P(("grp", "dev"), None),
            P(("grp", "dev"), None),
            P(None, ("grp", "dev")),
            P(),
            P(),
        ),
        out_specs=(P(("grp", "dev"), None), P(), P()),
        check_vma=False,
    )
```

```python
import functools
import math

import jax
import jax.numpy as jnp
from jax import lax
from jax.experimental import pallas as pl
from jax.experimental.pallas import tpu as pltpu
from jax.sharding import PartitionSpec as P

F32, BF16, I32 = jnp.float32, jnp.bfloat16, jnp.int32
LANES = 128
PAD = 112


def nt(a, b, **kw):
    return lax.dot_general(a, b, (((1,), (1,)), ((), ())), preferred_element_type=F32, **kw)


def tn(a, b, **kw):
    return lax.dot_general(a, b, (((0,), (0,)), ((), ())), preferred_element_type=F32, **kw)


def nn(a, b, **kw):
    return lax.dot_general(a, b, (((1,), (0,)), ((), ())), preferred_element_type=F32, **kw)


def split(x):
    top = x.astype(BF16)
    return top, (x - top.astype(F32)).astype(BF16)


def padded(x):
    more = -x.shape[0] % 16
    return jnp.concatenate([x, jnp.zeros((more, x.shape[1]), x.dtype)], axis=0) if more else x


def precise(product, a, b):
    rows = a.shape[0]
    a = padded(a)
    tall = a.shape[0]
    a_top, a_low = split(a)
    b_top, b_low = split(b)
    both = product(jnp.concatenate([a_top, a_low], axis=0), b_top)
    return (both[0:tall] + both[tall:] + product(a_top, b_low))[0:rows]


def params(mib=56):
    return pltpu.CompilerParams(vmem_limit_bytes=mib * 1024 * 1024)


def cost(flops, nbytes):
    return pl.CostEstimate(flops=flops, bytes_accessed=nbytes, transcendentals=0)


def hits(ids, rows, first):
    row = lax.broadcasted_iota(I32, (rows, ids.shape[1]), 0)
    return jnp.where(row == ids - first, 1.0, 0.0).astype(BF16)


def pick_negs_kernel(ids_ref, ent_ref, out_ref, acc_ref):
    step = pl.program_id(0)
    width = ent_ref.shape[1]
    part = nn(ent_ref[...], hits(ids_ref[...], width, step * width))

    @pl.when(step == 0)
    def _():
        acc_ref[...] = part

    @pl.when(step > 0)
    def _():
        acc_ref[...] += part

    @pl.when(step == pl.num_programs(0) - 1)
    def _():
        rows = acc_ref[...].astype(BF16)
        for k in range(out_ref.shape[0]):
            out_ref[k] = rows


def pick_negs(ids, ent_t, group):
    cols, ent = ent_t.shape
    width = 1024
    return pl.pallas_call(
        pick_negs_kernel,
        grid=(ent // width,),
        in_specs=[
            pl.BlockSpec((1, ids.shape[1]), lambda i: (0, 0)),
            pl.BlockSpec((cols, width), lambda i: (0, i)),
        ],
        out_specs=pl.BlockSpec((group, cols, ids.shape[1]), lambda i: (0, 0, 0)),
        out_shape=jax.ShapeDtypeStruct((group, cols, ids.shape[1]), BF16),
        scratch_shapes=[pltpu.VMEM((cols, ids.shape[1]), F32)],
        compiler_params=params(),
        cost_estimate=cost(2 * cols * ent * 128, cols * ent * 2),
        name="pick_negs",
    )(ids, ent_t)


def up_to_here():
    rows = lax.broadcasted_iota(I32, (LANES, LANES), 0)
    cols = lax.broadcasted_iota(I32, (LANES, LANES), 1)
    return jnp.where(rows <= cols, 1.0, 0.0).astype(BF16)


def up_to_here():
    rows = lax.broadcasted_iota(I32, (LANES, LANES), 0)
    cols = lax.broadcasted_iota(I32, (LANES, LANES), 1)
    return jnp.where(rows <= cols, 1.0, 0.0).astype(BF16)


def band(rows, slots):
    bands = LANES // slots
    return rows if bands == 1 else pl.cdiv(pl.cdiv(rows, bands), 16) * 16


def pick_coef_kernel(nrel, rel_ref, coef_ref, picked_ref, halves, acc):
    step = pl.program_id(0)
    nb, width = coef_ref.shape
    lane = lax.broadcasted_iota(I32, (nb, width), 1) + step * width
    block = jnp.where(lane < nrel, coef_ref[...], 0.0)
    low = block - block.astype(BF16).astype(F32)
    tall = acc.shape[0] // 2
    spare = [jnp.zeros((tall - nb, width), F32)] * (tall > nb)
    halves[...] = jnp.concatenate([block, *spare, low, *spare], axis=0).astype(BF16)

    @pl.when(step == 0)
    def _():
        acc[...] = jnp.zeros_like(acc)

    acc[...] += nn(halves[...], hits(rel_ref[...], width, step * width))

    @pl.when(step == pl.num_programs(0) - 1)
    def _():
        picked_ref[...] = acc[0:nb] + acc[tall:tall + nb]


def pick_coef(rel, coef_t):
    nb, nrel = coef_t.shape
    triples = rel.shape[1]
    width = 1920
    tall = pl.cdiv(nb, 8) * 8
    return pl.pallas_call(
        functools.partial(pick_coef_kernel, nrel),
        grid=(pl.cdiv(nrel, width),),
        in_specs=[
            pl.BlockSpec((1, triples), lambda i: (0, 0)),
            pl.BlockSpec((nb, width), lambda i: (0, i)),
        ],
        out_specs=pl.BlockSpec((nb, triples), lambda i: (0, 0)),
        out_shape=jax.ShapeDtypeStruct((nb, triples), F32),
        scratch_shapes=[pltpu.VMEM((2 * tall, width), BF16), pltpu.VMEM((2 * tall, triples), F32)],
        compiler_params=params(),
        cost_estimate=cost(4 * tall * nrel * triples, nb * nrel * 4),
        name="pick_coef",
    )(rel, coef_t)


def slot_of_relation(rel, devices, plan):
    span, slots, room = plan
    triples = rel.shape[1]
    number = lax.broadcasted_iota(I32, (devices, LANES), 0)
    later = lax.broadcasted_iota(I32, (LANES, triples), 1)
    row = lax.broadcasted_iota(I32, (LANES, triples), 0)
    seen = jnp.zeros((1, triples), F32)
    same = []
    for b in range(triples // LANES):
        down = jnp.broadcast_to(
            rel[:, b * LANES:(b + 1) * LANES].astype(F32), (LANES, LANES)).T[:, 0:1]
        equal = jnp.where(down.astype(I32) == rel, 1.0, 0.0)
        same.append(equal.astype(BF16))
        before = jnp.where(row + b * LANES < later, equal, 0.0)
        seen = seen + jnp.sum(before, axis=0, keepdims=True)
    first = jnp.where(seen == 0.0, 1.0, 0.0)
    summer = rel // span
    marks = []
    for b in range(triples // LANES):
        lanes = slice(b * LANES, (b + 1) * LANES)
        marks.append(jnp.where(number == summer[:, lanes], first[:, lanes], 0.0))
    sums = nn(jnp.concatenate(marks, axis=0).astype(BF16), up_to_here())
    carry = jnp.zeros((devices, 1), F32)
    lead = []
    for b, mark in enumerate(marks):
        part = sums[b * devices:(b + 1) * devices]
        lead.append(jnp.sum(mark * (part + carry - 1.0), axis=0, keepdims=True))
        carry = carry + part[:, LANES - 1:LANES]
    lead = jnp.minimum(jnp.concatenate(lead, axis=1), 255.0)
    lead = jnp.broadcast_to(lead, (16, triples)).astype(BF16)
    slot = nn(lead, jnp.concatenate(same, axis=0))[0:1].astype(I32)
    fits = slot < room
    place = jnp.where(fits, summer * slots + slot, -1)
    local = jnp.where(seen == 0.0, rel - summer * span, -1)
    over = jnp.max(jnp.where(fits, 0.0, 1.0), axis=1, keepdims=True)
    return place, local, over


def coef_blocks(rows, base, place, local, over, devices, plan, share):
    span, slots, room = plan
    nb = rows.shape[0]
    cols = base.shape[1]
    lanes = devices * slots

    def halves(block):
        spare = jnp.zeros((PAD - block.shape[0], block.shape[1]), F32)
        return jnp.concatenate(split(jnp.concatenate([block, spare], axis=0)), axis=0)

    high = local // 64
    pair = jnp.concatenate([high, local - high * 64], axis=0)
    pair = jnp.where(local >= 0, pair, 0).astype(F32)
    both = nt(halves(jnp.concatenate([rows, pair], axis=0)), hits(place, lanes, 0))
    column = lax.broadcasted_iota(I32, (1, cols), 1)
    owner = column // share
    spots = owner * slots + room + column - owner * share
    both = both + nt(halves(base), hits(spots, lanes, 0))
    row = lax.broadcasted_iota(I32, (PAD, lanes), 0)
    return jnp.where(row == nb + 2, over, both[0:PAD] + both[PAD:])


def score_kernel(neg_count, plan, share, rel_ref, picked_ref, negs_ref, head_ref, tail_ref,
                 row_ref, bases_ref, send_ref, grads_ref, rows_ref, base_ref, probs_ref, hrel_ref):
    group, cols, per = negs_ref.shape
    triples = head_ref.shape[1]
    devices, high, _ = send_ref.shape
    slots = plan[1]
    picked = picked_ref[...]
    vec = precise(nn, bases_ref[...], picked)
    head = head_ref[...].astype(F32)
    tail = tail_ref[...].astype(F32)
    head_vec = head * vec
    gate = jax.nn.sigmoid(-jnp.sum(head_vec * tail, axis=0, keepdims=True))
    head_rel = head_vec.astype(BF16)
    hrel_ref[...] = head_rel
    mix = jnp.zeros((cols, triples), F32)
    for first in range(0, group, 8):
        negs = jnp.concatenate([negs_ref[first + k] for k in range(8)], axis=1)
        probs = jax.nn.sigmoid(tn(negs, head_rel)).astype(BF16)
        probs_ref[first * per:(first + 8) * per] = probs
        mix = mix + nn(negs, probs)
    rel_grad = -gate * head * tail + head * mix / neg_count
    rows = precise(nn, bases_ref[...].T, rel_grad)
    base = precise(nt, picked, rel_grad)
    rows_ref[...] = rows
    base_ref[...] = base
    place, local, over = slot_of_relation(rel_ref[...], devices, plan)
    both = coef_blocks(rows, base, place, local, over, devices, plan, share)
    bands = LANES // slots
    if bands * high > PAD:
        spare = jnp.zeros((bands * high - PAD, both.shape[1]), F32)
        both = jnp.concatenate([both, spare], axis=0)
    for o in range(devices):
        block = [both[b * high:(b + 1) * high, o * slots:(o + 1) * slots] for b in range(bands)]
        send_ref[o] = jnp.concatenate(block, axis=1).astype(BF16)
    grads_ref[0:cols, 0:triples] = (-gate * vec * tail + vec * mix / neg_count).astype(BF16)
    grads_ref[0:cols, triples:] = (-gate * head * vec).astype(BF16)
    for side in range(2):
        ids = row_ref[side:side + 1]
        lanes = slice(side * triples, (side + 1) * triples)
        upper = ids // 64
        pair = jnp.concatenate([upper, ids - upper * 64], axis=0).astype(F32)
        more = grads_ref.shape[0] - cols - 2
        if more:
            pair = jnp.concatenate([pair, jnp.zeros((more, triples), F32)], axis=0)
        grads_ref[cols:, lanes] = pair.astype(BF16)


def score_step(rel, picked, negs, head_t, tail_t, rows, bases_t, tall, neg_count, devices, plan,
               share):
    group, cols, per = negs.shape
    triples = head_t.shape[1]
    nb = bases_t.shape[1]
    high = pl.cdiv(PAD * plan[1], 8 * LANES) * 8
    outs = [((devices, high, LANES), BF16), ((tall, 2 * triples), BF16), ((nb, triples), F32),
            ((nb, cols), F32), ((group * per, triples), BF16), ((cols, triples), BF16)]
    return pl.pallas_call(
        functools.partial(score_kernel, neg_count, plan, share),
        out_shape=[jax.ShapeDtypeStruct(s, d) for s, d in outs],
        compiler_params=params(),
        cost_estimate=cost(2 * cols * triples * 2 * group * per, 16 << 20),
        name="score_step",
    )(rel, picked, negs, head_t, tail_t, rows, bases_t)


def order_kernel(devices, slots, grads_ref, owner_ref, send_ref, pos):
    owners, high, _ = send_ref.shape
    bands = LANES // slots
    step = pl.program_id(0)

    @pl.when(step == 0)
    def _():
        owner = owner_ref[...]
        triples = owner.shape[1]
        number = lax.broadcasted_iota(I32, (devices, LANES), 0)
        parts, marks = [], []
        for side in range(2):
            for b in range(triples // LANES):
                part = owner[side:side + 1, b * LANES:(b + 1) * LANES]
                parts.append(part)
                marks.append(jnp.where(number == part, 1.0, 0.0))
        sums = nn(jnp.concatenate(marks, axis=0).astype(BF16), up_to_here())
        carry = jnp.zeros((devices, 1), F32)
        for b, (part, mark) in enumerate(zip(parts, marks)):
            here = sums[b * devices:(b + 1) * devices]
            slot = jnp.sum(mark * (here + carry), axis=0, keepdims=True) - 1.0
            pos[:, b * LANES:(b + 1) * LANES] = part * slots + slot.astype(I32)
            carry = carry + here[:, LANES - 1:LANES]

    part = nt(grads_ref[...], hits(pos[...], owners * slots, step * owners * slots))
    part = part.astype(BF16)
    for o in range(owners):
        at = o * slots
        block = [part[b * high:(b + 1) * high, at:at + slots] for b in range(bands)]
        send_ref[o] = jnp.concatenate(block, axis=1)


def order_slots(grads, owner_t, devices, slots, rows):
    owners = 512 // slots
    high = band(rows, slots)
    whole = lambda shape: pl.BlockSpec(shape, lambda i: (0,) * len(shape))
    return pl.pallas_call(
        functools.partial(order_kernel, devices, slots),
        grid=(devices // owners,),
        in_specs=[whole(grads.shape), whole(owner_t.shape)],
        out_specs=pl.BlockSpec((owners, high, LANES), lambda i: (i, 0, 0)),
        out_shape=jax.ShapeDtypeStruct((devices, high, LANES), BF16),
        scratch_shapes=[pltpu.VMEM((1, grads.shape[1]), I32)],
        compiler_params=params(),
        cost_estimate=cost(rows * grads.shape[1] * devices * slots * 2, 4 << 20),
        name="order_slots",
    )(grads, owner_t)


def partial_kernel(neg_count, me_ref, probs_ref, hrel_ref, parts_ref, block):
    half, per = parts_ref.shape[1], parts_ref.shape[3]
    for first in range(0, 2 * half, 8):
        part = nt(hrel_ref[...], probs_ref[first * per:(first + 8) * per]) / neg_count
        block[...] = part
        for k in range(8):
            lane = pl.multiple_of((k ^ me_ref[0]) * per, per)
            parts_ref[k % 2, (first + k) // 2] = block[:, pl.ds(lane, per)].astype(BF16)


def partial_step(me, probs, hrel, group, neg_count):
    cols = hrel.shape[0]
    whole = lambda shape: pl.BlockSpec(shape, lambda i, me: (0,) * len(shape))
    shape = (2, group // 2, cols, LANES)
    return pl.pallas_call(
        functools.partial(partial_kernel, neg_count),
        grid_spec=pltpu.PrefetchScalarGridSpec(
            num_scalar_prefetch=1,
            grid=(1,),
            in_specs=[whole(probs.shape), whole(hrel.shape)],
            out_specs=whole(shape),
            scratch_shapes=[pltpu.VMEM((cols, 8 * LANES), F32)],
        ),
        out_shape=jax.ShapeDtypeStruct(shape, BF16),
        compiler_params=params(),
        cost_estimate=cost(1, 1),
        name="partial_step",
    )(me, probs, hrel)


def coef_sum_kernel(nb, plan, recv_ref, out_ref, flag_ref, left):
    span, slots, room = plan
    sources, high, _ = recv_ref.shape
    bands = LANES // slots
    for s in range(0, sources, bands):
        lanes = slice(s * slots, (s + bands) * slots)
        tall = []
        for b in range(bands):
            block = [recv_ref[s + k, :, b * slots:(b + 1) * slots] for k in range(bands)]
            tall.append(jnp.concatenate(block, axis=1).astype(F32))
        left[:, lanes] = jnp.concatenate(tall, axis=0)[0:PAD].astype(BF16)
    extra = left[PAD - 16:PAD].astype(F32)
    at = nb - (PAD - 16)
    ids = (extra[at:at + 1] * 64.0 + extra[at + 1:at + 2]).astype(I32)
    lane = lax.broadcasted_iota(I32, ids.shape, 1)
    lane = lane - lane // slots * slots
    ids = jnp.where(lane < room, ids, span + lane - room)
    total = nt(left[0:PAD], hits(ids, out_ref.shape[1], 0))
    out_ref[...] = total[0:nb].astype(BF16)
    over = jnp.max(extra[at + 2:at + 3], axis=1, keepdims=True)
    flag_ref[...] = jnp.broadcast_to(over, flag_ref.shape).astype(I32)


def coef_sum(recv, nb, plan, width):
    sources = recv.shape[0]
    slots = plan[1]
    return pl.pallas_call(
        functools.partial(coef_sum_kernel, nb, plan),
        out_shape=[jax.ShapeDtypeStruct((nb, width), BF16), jax.ShapeDtypeStruct((1, LANES), I32)],
        scratch_shapes=[pltpu.VMEM((PAD, sources * slots), BF16)],
        compiler_params=params(20),
        cost_estimate=cost(1, 1),
        name="coef_sum",
    )(recv)


def spread_kernel(span, share, place_ref, *refs):
    sets, (coef_ref, base_ref, pieces, strips) = refs[:-4], refs[-4:]
    step = pl.program_id(0)
    group, layers, nb, _ = pieces.shape

    @pl.when(step == 0)
    def _():
        number = 0
        for ref in sets:
            for s in range(ref.shape[0]):
                pieces[number ^ place_ref[0]] = ref[s]
                number += 1

    slab = lax.rem(place_ref[1] - step + layers, layers)
    row = [pieces[k, slab].astype(F32) for k in range(group)]
    coef_ref[...] = jnp.concatenate([r[:, 0:span] for r in row], axis=1)
    strip = jnp.concatenate([r[:, span:span + share] for r in row], axis=1)
    strips[step] = jnp.concatenate([strip, jnp.zeros((PAD - nb, strip.shape[1]), F32)], axis=0)

    @pl.when(step == layers - 1)
    def _():
        whole = jnp.concatenate([strips[g] for g in range(layers)], axis=1)
        base_ref[...] = whole[0:nb, 0:base_ref.shape[0]].T


def spread(me, layer, sets, span, share, nrel, cols):
    group = sum(s.shape[0] for s in sets)
    _, layers, nb, width = sets[0].shape
    whole = lambda shape: pl.BlockSpec(shape, lambda i, place: (0,) * len(shape))
    return pl.pallas_call(
        functools.partial(spread_kernel, span, share),
        grid_spec=pltpu.PrefetchScalarGridSpec(
            num_scalar_prefetch=1,
            grid=(layers,),
            in_specs=[whole(s.shape) for s in sets],
            out_specs=[
                pl.BlockSpec((nb, group * span), lambda i, place: (0, i)),
                whole((cols, nb)),
            ],
            scratch_shapes=[pltpu.VMEM((group, layers, nb, width), BF16),
                            pltpu.VMEM((layers, PAD, group * share), F32)],
        ),
        out_shape=[jax.ShapeDtypeStruct((nb, nrel), F32), jax.ShapeDtypeStruct((cols, nb), F32)],
        compiler_params=params(),
        cost_estimate=cost(1, 1),
        name="spread",
    )(jnp.concatenate([me, layer]), *sets)


def add_rows_kernel(slots, recv_ref, neg_ref, *refs):
    part_refs, (out_ref, grads, ids, sems) = refs[:-4], refs[-4:]
    step = pl.program_id(0)
    cols, width = out_ref.shape
    sources, high, _ = recv_ref.shape
    bands = LANES // slots
    lanes = sources * slots

    @pl.when(step == 0)
    def _():
        copies = []
        if bands == 1:
            for s in range(sources):
                to = grads.at[:, s * slots:(s + 1) * slots]
                copies.append(pltpu.make_async_copy(recv_ref.at[s], to, sems.at[s]))
        else:
            for s in range(0, sources, bands):
                at = slice(s * slots, (s + bands) * slots)
                for b in range(bands):
                    block = [recv_ref[s + k, :, b * slots:(b + 1) * slots] for k in range(bands)]
                    grads[b * high:(b + 1) * high, at] = jnp.concatenate(block, axis=1)
        for copy in copies:
            copy.start()
        total = jnp.zeros((cols, LANES), F32)
        for ref in part_refs:
            for k in range(ref.shape[0]):
                total = total + ref[k].astype(F32)
        top, low = split(total)
        grads[0:cols, lanes:lanes + LANES] = top
        grads[0:cols, lanes + LANES:] = low
        ids[:, lanes:lanes + LANES] = neg_ref[...]
        ids[:, lanes + LANES:] = neg_ref[...]
        for copy in copies:
            copy.wait()
        pair = grads[cols:cols + 2, 0:lanes].astype(F32)
        ids[:, 0:lanes] = (pair[0:1] * 64.0 + pair[1:2]).astype(I32)

    out_ref[...] = nt(grads[0:cols], hits(ids[...], width, step * width))


def add_rows(recv, slots, cols, ent, neg_ids, part_sets):
    sources, high, _ = recv.shape
    bands = LANES // slots
    width = 1024
    lanes = sources * slots + 2 * LANES
    whole = lambda shape: pl.BlockSpec(shape, lambda i: (0,) * len(shape))
    there = pl.BlockSpec(memory_space=pl.ANY) if bands == 1 else whole(recv.shape)
    return pl.pallas_call(
        functools.partial(add_rows_kernel, slots),
        grid=(ent // width,),
        in_specs=[there] + [whole(r.shape) for r in (neg_ids, *part_sets)],
        out_specs=pl.BlockSpec((cols, width), lambda i: (0, i)),
        out_shape=jax.ShapeDtypeStruct((cols, ent), F32),
        scratch_shapes=[pltpu.VMEM((bands * high, lanes), BF16),
                        pltpu.VMEM((1, lanes), I32),
                        pltpu.SemaphoreType.DMA((sources,))],
        compiler_params=params(32),
        cost_estimate=cost(1, 1),
        name="add_rows",
    )(recv, neg_ids, *part_sets)


def from_group(block, group):
    block = block[None]
    if group != 8:
        return [lax.all_gather(block, "dev", axis=0, tiled=True)]
    swap = lambda x, far: lax.ppermute(x, "dev", [(i, i ^ far) for i in range(group)])
    blocks = {0: block, 2: swap(block, 2), 4: swap(block, 4), 6: swap(block, 6)}
    for far in (0, 2, 4, 6):
        blocks[far + 1] = swap(blocks[far], 1)
    return [blocks[t] for t in range(group)]


def sum_here(parts, group):
    if group != 8:
        parts = parts.swapaxes(0, 1).reshape((group,) + parts.shape[2:])
        return [lax.all_to_all(parts, "dev", 0, 0, tiled=True)]
    swap = lambda x, far: lax.ppermute(x, "dev", [(i, i ^ far) for i in range(group)])
    pairs = parts[0].astype(F32) + swap(parts[1], 1).astype(F32)
    pairs = pairs.astype(BF16)
    return [pairs[0:1]] + [swap(pairs[n:n + 1], 2 * n) for n in (1, 2, 3)]


def shift_layers(block, far, layers):
    return lax.ppermute(block, "grp", [(i, (i + far) % layers) for i in range(layers)])


def everywhere(values):
    for axis in ("dev", "grp"):
        count = lax.axis_size(axis)
        ring = [(i, (i + 1) % count) for i in range(count)]

        def turn(_, state):
            near = tuple(lax.ppermute(v, axis, ring) for v in state[0])
            return near, tuple(t + n for t, n in zip(state[1], near))

        values = lax.fori_loop(0, count - 1, turn, (values, values))[1]
    return values


def per_device(head_emb, tail_emb, relation, owners, owner_rows, entities, neg_rows, coef, bases):
    triples, cols = head_emb.shape
    group = lax.axis_size("dev")
    layers = lax.axis_size("grp")
    devices = layers * group
    neg_count = neg_rows.shape[1] * group
    ent_local = entities.shape[0]
    nrel, nb = coef.shape
    cap = 4 * triples // devices
    tall = LANES // cap * band(cols + 2, cap)
    share = pl.cdiv(cols, devices)
    step = LANES // math.gcd(group, LANES)
    span = pl.cdiv(pl.cdiv(nrel, devices), step) * step
    slots = 2 * triples // devices
    plan = (span, slots, slots - share)
    width = pl.cdiv(span + share, LANES) * LANES

    head_t, tail_t, owner_t, row_t = head_emb.T, tail_emb.T, owners.T, owner_rows.T
    coef_t, bases_t = coef.T, bases.T
    rel = relation.reshape(1, triples)

    sent_negs = pick_negs(neg_rows, entities.T, group)
    negs = lax.all_to_all(sent_negs, "dev", 0, 0, tiled=True)
    picked = pick_coef(rel, coef_t)
    coef_send, grads, rows, base, probs, hrel = score_step(
        rel, picked, negs, head_t, tail_t, row_t, bases_t, tall, neg_count, devices, plan, share)
    coef_recv = lax.all_to_all(coef_send, ("grp", "dev"), 0, 0, tiled=True)
    send = order_slots(grads, owner_t, devices, cap, cols + 2)
    send, coef_recv = lax.optimization_barrier((send, coef_recv))
    piece, flag = coef_sum(coef_recv, nb, plan, width)
    slabs = [piece] + [shift_layers(piece, far, layers) for far in range(1, layers)]
    send, slabs = lax.optimization_barrier((send, slabs))
    recv = lax.all_to_all(send, ("grp", "dev"), 0, 0, tiled=True)

    me = lax.axis_index("dev").astype(I32).reshape(1)
    layer = lax.axis_index("grp").astype(I32).reshape(1)
    at = me if group == 8 else jnp.zeros((1,), I32)
    pieces = from_group(jnp.stack(slabs), group)

    def packed():
        return tuple(spread(at, layer, pieces, span, share, nrel, cols))

    def dense():
        return everywhere((jnp.zeros((nb, nrel), F32).at[:, relation].add(rows), base.T))

    parts = sum_here(partial_step(at, probs, hrel, group, neg_count), group)
    parts, pieces = lax.optimization_barrier((parts, pieces))
    coef_grad, bases_grad = lax.cond(flag[0, 0] == 0, packed, dense)
    ent_grad = add_rows(recv, cap, cols, ent_local, neg_rows, parts)
    return ent_grad.T, coef_grad.T, bases_grad.T


def solution(mesh):
    return jax.shard_map(
        per_device,
        mesh=mesh,
        in_specs=(
            P(("grp", "dev"), None),
            P(("grp", "dev"), None),
            P(("grp", "dev")),
            P(("grp", "dev"), None),
            P(("grp", "dev"), None),
            P(("grp", "dev"), None),
            P(None, ("grp", "dev")),
            P(),
            P(),
        ),
        out_specs=(P(("grp", "dev"), None), P(), P()),
        check_vma=False,
    )
```

```python
import functools
import math

import jax
import jax.numpy as jnp
from jax import lax
from jax.experimental import pallas as pl
from jax.experimental.pallas import tpu as pltpu
from jax.sharding import PartitionSpec as P

F32, BF16, I32 = jnp.float32, jnp.bfloat16, jnp.int32
LANES = 128
PAD = 112


def nt(a, b, **kw):
    return lax.dot_general(a, b, (((1,), (1,)), ((), ())), preferred_element_type=F32, **kw)


def tn(a, b, **kw):
    return lax.dot_general(a, b, (((0,), (0,)), ((), ())), preferred_element_type=F32, **kw)


def nn(a, b, **kw):
    return lax.dot_general(a, b, (((1,), (0,)), ((), ())), preferred_element_type=F32, **kw)


def split(x):
    top = x.astype(BF16)
    return top, (x - top.astype(F32)).astype(BF16)


def padded(x):
    more = -x.shape[0] % 16
    return jnp.concatenate([x, jnp.zeros((more, x.shape[1]), x.dtype)], axis=0) if more else x


def precise(product, a, b):
    rows = a.shape[0]
    a = padded(a)
    tall = a.shape[0]
    a_top, a_low = split(a)
    b_top, b_low = split(b)
    both = product(jnp.concatenate([a_top, a_low], axis=0), b_top)
    return (both[0:tall] + both[tall:] + product(a_top, b_low))[0:rows]


def params(mib=56):
    return pltpu.CompilerParams(vmem_limit_bytes=mib * 1024 * 1024)


def cost(flops, nbytes):
    return pl.CostEstimate(flops=flops, bytes_accessed=nbytes, transcendentals=0)


def hits(ids, rows, first):
    row = lax.broadcasted_iota(I32, (rows, ids.shape[1]), 0)
    return jnp.where(row == ids - first, 1.0, 0.0).astype(BF16)


def pick_negs_kernel(ids_ref, ent_ref, out_ref, acc_ref):
    step = pl.program_id(0)
    width = ent_ref.shape[1]
    part = nn(ent_ref[...], hits(ids_ref[...], width, step * width))

    @pl.when(step == 0)
    def _():
        acc_ref[...] = part

    @pl.when(step > 0)
    def _():
        acc_ref[...] += part

    @pl.when(step == pl.num_programs(0) - 1)
    def _():
        rows = acc_ref[...].astype(BF16)
        for k in range(out_ref.shape[0]):
            out_ref[k] = rows


def pick_negs(ids, ent_t, group):
    cols, ent = ent_t.shape
    width = 1024
    return pl.pallas_call(
        pick_negs_kernel,
        grid=(ent // width,),
        in_specs=[
            pl.BlockSpec((1, ids.shape[1]), lambda i: (0, 0)),
            pl.BlockSpec((cols, width), lambda i: (0, i)),
        ],
        out_specs=pl.BlockSpec((group, cols, ids.shape[1]), lambda i: (0, 0, 0)),
        out_shape=jax.ShapeDtypeStruct((group, cols, ids.shape[1]), BF16),
        scratch_shapes=[pltpu.VMEM((cols, ids.shape[1]), F32)],
        compiler_params=params(),
        cost_estimate=cost(2 * cols * ent * 128, cols * ent * 2),
        name="pick_negs",
    )(ids, ent_t)


def up_to_here():
    rows = lax.broadcasted_iota(I32, (LANES, LANES), 0)
    cols = lax.broadcasted_iota(I32, (LANES, LANES), 1)
    return jnp.where(rows <= cols, 1.0, 0.0).astype(BF16)


def up_to_here():
    rows = lax.broadcasted_iota(I32, (LANES, LANES), 0)
    cols = lax.broadcasted_iota(I32, (LANES, LANES), 1)
    return jnp.where(rows <= cols, 1.0, 0.0).astype(BF16)


def band(rows, slots):
    bands = LANES // slots
    return rows if bands == 1 else pl.cdiv(pl.cdiv(rows, bands), 16) * 16


def pick_coef_kernel(nrel, fold, rel_ref, coef_ref, picked_ref, halves, acc):
    step = pl.program_id(0)
    nb, width = coef_ref.shape
    part = width // fold
    tall = acc.shape[0]
    half = tall // 2
    lane = lax.broadcasted_iota(I32, (nb, part), 1) + step * width
    spare = [jnp.zeros((half - nb, part), F32)] * (half > nb)
    for f in range(fold):
        block = coef_ref[:, f * part:(f + 1) * part]
        block = jnp.where(lane < nrel - f * part, block, 0.0)
        low = block - block.astype(BF16).astype(F32)
        both = jnp.concatenate([block, *spare, low, *spare], axis=0)
        halves[f * tall:(f + 1) * tall] = both.astype(BF16)
    here = rel_ref[...] - step * width
    where = here // part
    here = jnp.where((here >= 0) & (here < width), here - where * part, -1)
    found = nn(halves[...], hits(here, part, 0))
    total = jnp.where(where == 0, found[0:tall], 0.0)
    for f in range(1, fold):
        total = jnp.where(where == f, found[f * tall:(f + 1) * tall], total)

    @pl.when(step == 0)
    def _():
        acc[...] = total

    @pl.when(step > 0)
    def _():
        acc[...] += total

    @pl.when(step == pl.num_programs(0) - 1)
    def _():
        picked_ref[...] = acc[0:nb] + acc[half:half + nb]


def pick_coef(rel, coef_t):
    nb, nrel = coef_t.shape
    triples = rel.shape[1]
    fold = 2
    width = fold * 1920
    tall = 2 * (pl.cdiv(nb, 8) * 8)
    return pl.pallas_call(
        functools.partial(pick_coef_kernel, nrel, fold),
        grid=(pl.cdiv(nrel, width),),
        in_specs=[
            pl.BlockSpec((1, triples), lambda i: (0, 0)),
            pl.BlockSpec((nb, width), lambda i: (0, i)),
        ],
        out_specs=pl.BlockSpec((nb, triples), lambda i: (0, 0)),
        out_shape=jax.ShapeDtypeStruct((nb, triples), F32),
        scratch_shapes=[pltpu.VMEM((fold * tall, width // fold), BF16),
                        pltpu.VMEM((tall, triples), F32)],
        compiler_params=params(),
        cost_estimate=cost(2 * tall * nrel * triples, nb * nrel * 4),
        name="pick_coef",
    )(rel, coef_t)


def slot_of_relation(rel, devices, plan):
    span, slots, room = plan
    triples = rel.shape[1]
    number = lax.broadcasted_iota(I32, (devices, LANES), 0)
    later = lax.broadcasted_iota(I32, (LANES, triples), 1)
    row = lax.broadcasted_iota(I32, (LANES, triples), 0)
    seen = jnp.zeros((1, triples), F32)
    same = []
    for b in range(triples // LANES):
        down = jnp.broadcast_to(
            rel[:, b * LANES:(b + 1) * LANES].astype(F32), (LANES, LANES)).T[:, 0:1]
        equal = jnp.where(down.astype(I32) == rel, 1.0, 0.0)
        same.append(equal.astype(BF16))
        before = jnp.where(row + b * LANES < later, equal, 0.0)
        seen = seen + jnp.sum(before, axis=0, keepdims=True)
    first = jnp.where(seen == 0.0, 1.0, 0.0)
    summer = rel // span
    marks = []
    for b in range(triples // LANES):
        lanes = slice(b * LANES, (b + 1) * LANES)
        marks.append(jnp.where(number == summer[:, lanes], first[:, lanes], 0.0))
    sums = nn(jnp.concatenate(marks, axis=0).astype(BF16), up_to_here())
    carry = jnp.zeros((devices, 1), F32)
    lead = []
    for b, mark in enumerate(marks):
        part = sums[b * devices:(b + 1) * devices]
        lead.append(jnp.sum(mark * (part + carry - 1.0), axis=0, keepdims=True))
        carry = carry + part[:, LANES - 1:LANES]
    lead = jnp.minimum(jnp.concatenate(lead, axis=1), 255.0)
    lead = jnp.broadcast_to(lead, (16, triples)).astype(BF16)
    slot = nn(lead, jnp.concatenate(same, axis=0))[0:1].astype(I32)
    fits = slot < room
    place = jnp.where(fits, summer * slots + slot, -1)
    local = jnp.where(seen == 0.0, rel - summer * span, -1)
    over = jnp.max(jnp.where(fits, 0.0, 1.0), axis=1, keepdims=True)
    return place, local, over


def coef_blocks(rows, base, place, local, over, devices, plan, share):
    span, slots, room = plan
    nb = rows.shape[0]
    cols = base.shape[1]
    lanes = devices * slots

    def halves(block):
        spare = jnp.zeros((PAD - block.shape[0], block.shape[1]), F32)
        return jnp.concatenate(split(jnp.concatenate([block, spare], axis=0)), axis=0)

    high = local // 64
    pair = jnp.concatenate([high, local - high * 64], axis=0)
    pair = jnp.where(local >= 0, pair, 0).astype(F32)
    both = nt(halves(jnp.concatenate([rows, pair], axis=0)), hits(place, lanes, 0))
    column = lax.broadcasted_iota(I32, (1, cols), 1)
    owner = column // share
    spots = owner * slots + room + column - owner * share
    both = both + nt(halves(base), hits(spots, lanes, 0))
    row = lax.broadcasted_iota(I32, (PAD, lanes), 0)
    return jnp.where(row == nb + 2, over, both[0:PAD] + both[PAD:])


def score_kernel(neg_count, plan, share, rel_ref, picked_ref, negs_ref, head_ref, tail_ref,
                 row_ref, bases_ref, send_ref, grads_ref, rows_ref, base_ref, probs_ref, hrel_ref):
    group, cols, per = negs_ref.shape
    triples = head_ref.shape[1]
    devices, high, _ = send_ref.shape
    slots = plan[1]
    picked = picked_ref[...]
    vec = precise(nn, bases_ref[...], picked)
    head = head_ref[...].astype(F32)
    tail = tail_ref[...].astype(F32)
    head_vec = head * vec
    gate = jax.nn.sigmoid(-jnp.sum(head_vec * tail, axis=0, keepdims=True))
    head_rel = head_vec.astype(BF16)
    hrel_ref[...] = head_rel
    mix = jnp.zeros((cols, triples), F32)
    for first in range(0, group, 8):
        negs = jnp.concatenate([negs_ref[first + k] for k in range(8)], axis=1)
        probs = (0.5 * jnp.tanh(0.5 * tn(negs, head_rel)) + 0.5).astype(BF16)
        probs_ref[first * per:(first + 8) * per] = probs
        mix = mix + nn(negs, probs)
    rel_grad = -gate * head * tail + head * mix / neg_count
    rows = precise(nn, bases_ref[...].T, rel_grad)
    base = precise(nt, picked, rel_grad)
    rows_ref[...] = rows
    base_ref[...] = base
    place, local, over = slot_of_relation(rel_ref[...], devices, plan)
    both = coef_blocks(rows, base, place, local, over, devices, plan, share)
    bands = LANES // slots
    if bands * high > PAD:
        spare = jnp.zeros((bands * high - PAD, both.shape[1]), F32)
        both = jnp.concatenate([both, spare], axis=0)
    for o in range(devices):
        block = [both[b * high:(b + 1) * high, o * slots:(o + 1) * slots] for b in range(bands)]
        send_ref[o] = jnp.concatenate(block, axis=1).astype(BF16)
    grads_ref[0:cols, 0:triples] = (-gate * vec * tail + vec * mix / neg_count).astype(BF16)
    grads_ref[0:cols, triples:] = (-gate * head * vec).astype(BF16)
    for side in range(2):
        ids = row_ref[side:side + 1]
        lanes = slice(side * triples, (side + 1) * triples)
        upper = ids // 64
        pair = jnp.concatenate([upper, ids - upper * 64], axis=0).astype(F32)
        more = grads_ref.shape[0] - cols - 2
        if more:
            pair = jnp.concatenate([pair, jnp.zeros((more, triples), F32)], axis=0)
        grads_ref[cols:, lanes] = pair.astype(BF16)


def score_step(rel, picked, negs, head_t, tail_t, rows, bases_t, tall, neg_count, devices, plan,
               share):
    group, cols, per = negs.shape
    triples = head_t.shape[1]
    nb = bases_t.shape[1]
    high = pl.cdiv(PAD * plan[1], 8 * LANES) * 8
    outs = [((devices, high, LANES), BF16), ((tall, 2 * triples), BF16), ((nb, triples), F32),
            ((nb, cols), F32), ((group * per, triples), BF16), ((cols, triples), BF16)]
    return pl.pallas_call(
        functools.partial(score_kernel, neg_count, plan, share),
        out_shape=[jax.ShapeDtypeStruct(s, d) for s, d in outs],
        compiler_params=params(),
        cost_estimate=cost(2 * cols * triples * 2 * group * per, 16 << 20),
        name="score_step",
    )(rel, picked, negs, head_t, tail_t, rows, bases_t)


def order_kernel(devices, slots, grads_ref, owner_ref, send_ref, pos):
    owners, high, _ = send_ref.shape
    bands = LANES // slots
    step = pl.program_id(0)

    @pl.when(step == 0)
    def _():
        owner = owner_ref[...]
        triples = owner.shape[1]
        number = lax.broadcasted_iota(I32, (devices, LANES), 0)
        parts, marks = [], []
        for side in range(2):
            for b in range(triples // LANES):
                part = owner[side:side + 1, b * LANES:(b + 1) * LANES]
                parts.append(part)
                marks.append(jnp.where(number == part, 1.0, 0.0))
        sums = nn(jnp.concatenate(marks, axis=0).astype(BF16), up_to_here())
        carry = jnp.zeros((devices, 1), F32)
        for b, (part, mark) in enumerate(zip(parts, marks)):
            here = sums[b * devices:(b + 1) * devices]
            slot = jnp.sum(mark * (here + carry), axis=0, keepdims=True) - 1.0
            pos[:, b * LANES:(b + 1) * LANES] = part * slots + slot.astype(I32)
            carry = carry + here[:, LANES - 1:LANES]

    part = nt(grads_ref[...], hits(pos[...], owners * slots, step * owners * slots))
    part = part.astype(BF16)
    for o in range(owners):
        at = o * slots
        block = [part[b * high:(b + 1) * high, at:at + slots] for b in range(bands)]
        send_ref[o] = jnp.concatenate(block, axis=1)


def order_slots(grads, owner_t, devices, slots, rows):
    owners = 512 // slots
    high = band(rows, slots)
    whole = lambda shape: pl.BlockSpec(shape, lambda i: (0,) * len(shape))
    return pl.pallas_call(
        functools.partial(order_kernel, devices, slots),
        grid=(devices // owners,),
        in_specs=[whole(grads.shape), whole(owner_t.shape)],
        out_specs=pl.BlockSpec((owners, high, LANES), lambda i: (i, 0, 0)),
        out_shape=jax.ShapeDtypeStruct((devices, high, LANES), BF16),
        scratch_shapes=[pltpu.VMEM((1, grads.shape[1]), I32)],
        compiler_params=params(),
        cost_estimate=cost(rows * grads.shape[1] * devices * slots * 2, 4 << 20),
        name="order_slots",
    )(grads, owner_t)


def partial_kernel(neg_count, me_ref, probs_ref, hrel_ref, parts_ref, block):
    half, per = parts_ref.shape[1], parts_ref.shape[3]
    for first in range(0, 2 * half, 8):
        part = nt(hrel_ref[...], probs_ref[first * per:(first + 8) * per]) / neg_count
        block[...] = part
        for k in range(8):
            lane = pl.multiple_of((k ^ me_ref[0]) * per, per)
            parts_ref[k % 2, (first + k) // 2] = block[:, pl.ds(lane, per)].astype(BF16)


def partial_step(me, probs, hrel, group, neg_count):
    cols = hrel.shape[0]
    whole = lambda shape: pl.BlockSpec(shape, lambda i, me: (0,) * len(shape))
    shape = (2, group // 2, cols, LANES)
    return pl.pallas_call(
        functools.partial(partial_kernel, neg_count),
        grid_spec=pltpu.PrefetchScalarGridSpec(
            num_scalar_prefetch=1,
            grid=(1,),
            in_specs=[whole(probs.shape), whole(hrel.shape)],
            out_specs=whole(shape),
            scratch_shapes=[pltpu.VMEM((cols, 8 * LANES), F32)],
        ),
        out_shape=jax.ShapeDtypeStruct(shape, BF16),
        compiler_params=params(),
        cost_estimate=cost(1, 1),
        name="partial_step",
    )(me, probs, hrel)


def coef_sum_kernel(nb, plan, recv_ref, out_ref, flag_ref, left):
    span, slots, room = plan
    sources, high, _ = recv_ref.shape
    bands = LANES // slots
    for s in range(0, sources, bands):
        lanes = slice(s * slots, (s + bands) * slots)
        tall = []
        for b in range(bands):
            block = [recv_ref[s + k, :, b * slots:(b + 1) * slots] for k in range(bands)]
            tall.append(jnp.concatenate(block, axis=1).astype(F32))
        left[:, lanes] = jnp.concatenate(tall, axis=0)[0:PAD].astype(BF16)
    extra = left[PAD - 16:PAD].astype(F32)
    at = nb - (PAD - 16)
    ids = (extra[at:at + 1] * 64.0 + extra[at + 1:at + 2]).astype(I32)
    lane = lax.broadcasted_iota(I32, ids.shape, 1)
    lane = lane - lane // slots * slots
    ids = jnp.where(lane < room, ids, span + lane - room)
    total = nt(left[0:PAD], hits(ids, out_ref.shape[1], 0))
    out_ref[...] = total[0:nb].astype(BF16)
    over = jnp.max(extra[at + 2:at + 3], axis=1, keepdims=True)
    flag_ref[...] = jnp.broadcast_to(over, flag_ref.shape).astype(I32)


def coef_sum(recv, nb, plan, width):
    sources = recv.shape[0]
    slots = plan[1]
    return pl.pallas_call(
        functools.partial(coef_sum_kernel, nb, plan),
        out_shape=[jax.ShapeDtypeStruct((nb, width), BF16), jax.ShapeDtypeStruct((1, LANES), I32)],
        scratch_shapes=[pltpu.VMEM((PAD, sources * slots), BF16)],
        compiler_params=params(20),
        cost_estimate=cost(1, 1),
        name="coef_sum",
    )(recv)


def spread_kernel(span, share, place_ref, *refs):
    sets, (coef_ref, base_ref, pieces, strips) = refs[:-4], refs[-4:]
    step = pl.program_id(0)
    group, layers, nb, _ = pieces.shape

    @pl.when(step == 0)
    def _():
        number = 0
        for ref in sets:
            for s in range(ref.shape[0]):
                pieces[number ^ place_ref[0]] = ref[s]
                number += 1

    slab = lax.rem(place_ref[1] - step + layers, layers)
    row = [pieces[k, slab].astype(F32) for k in range(group)]
    coef_ref[...] = jnp.concatenate([r[:, 0:span] for r in row], axis=1)
    strip = jnp.concatenate([r[:, span:span + share] for r in row], axis=1)
    strips[step] = jnp.concatenate([strip, jnp.zeros((PAD - nb, strip.shape[1]), F32)], axis=0)

    @pl.when(step == layers - 1)
    def _():
        whole = jnp.concatenate([strips[g] for g in range(layers)], axis=1)
        base_ref[...] = whole[0:nb, 0:base_ref.shape[0]].T


def spread(me, layer, sets, span, share, nrel, cols):
    group = sum(s.shape[0] for s in sets)
    _, layers, nb, width = sets[0].shape
    whole = lambda shape: pl.BlockSpec(shape, lambda i, place: (0,) * len(shape))
    return pl.pallas_call(
        functools.partial(spread_kernel, span, share),
        grid_spec=pltpu.PrefetchScalarGridSpec(
            num_scalar_prefetch=1,
            grid=(layers,),
            in_specs=[whole(s.shape) for s in sets],
            out_specs=[
                pl.BlockSpec((nb, group * span), lambda i, place: (0, i)),
                whole((cols, nb)),
            ],
            scratch_shapes=[pltpu.VMEM((group, layers, nb, width), BF16),
                            pltpu.VMEM((layers, PAD, group * share), F32)],
        ),
        out_shape=[jax.ShapeDtypeStruct((nb, nrel), F32), jax.ShapeDtypeStruct((cols, nb), F32)],
        compiler_params=params(),
        cost_estimate=cost(1, 1),
        name="spread",
    )(jnp.concatenate([me, layer]), *sets)


def add_rows_kernel(slots, recv_ref, neg_ref, own_ref, out_ref, grads, ids, sems):
    step = pl.program_id(0)
    cols, width = out_ref.shape
    sources, high, _ = recv_ref.shape
    bands = LANES // slots
    lanes = sources * slots

    @pl.when(step == 0)
    def _():
        copies = []
        if bands == 1:
            for s in range(sources):
                to = grads.at[:, s * slots:(s + 1) * slots]
                copies.append(pltpu.make_async_copy(recv_ref.at[s], to, sems.at[s]))
        else:
            for s in range(0, sources, bands):
                at = slice(s * slots, (s + bands) * slots)
                for b in range(bands):
                    block = [recv_ref[s + k, :, b * slots:(b + 1) * slots] for k in range(bands)]
                    grads[b * high:(b + 1) * high, at] = jnp.concatenate(block, axis=1)
        for copy in copies:
            copy.start()
        top, low = split(own_ref[...])
        grads[0:cols, lanes:lanes + LANES] = top
        grads[0:cols, lanes + LANES:] = low
        ids[:, lanes:lanes + LANES] = neg_ref[...]
        ids[:, lanes + LANES:] = neg_ref[...]
        for copy in copies:
            copy.wait()
        pair = grads[cols:cols + 2, 0:lanes].astype(F32)
        ids[:, 0:lanes] = (pair[0:1] * 64.0 + pair[1:2]).astype(I32)

    out_ref[...] = nt(grads[0:cols], hits(ids[...], width, step * width))


def add_rows(recv, slots, cols, ent, neg_ids, own_neg):
    sources, high, _ = recv.shape
    bands = LANES // slots
    width = 1024
    lanes = sources * slots + 2 * LANES
    whole = lambda shape: pl.BlockSpec(shape, lambda i: (0,) * len(shape))
    there = pl.BlockSpec(memory_space=pl.ANY) if bands == 1 else whole(recv.shape)
    return pl.pallas_call(
        functools.partial(add_rows_kernel, slots),
        grid=(ent // width,),
        in_specs=[there, whole(neg_ids.shape), whole(own_neg.shape)],
        out_specs=pl.BlockSpec((cols, width), lambda i: (0, i)),
        out_shape=jax.ShapeDtypeStruct((cols, ent), F32),
        scratch_shapes=[pltpu.VMEM((bands * high, lanes), BF16),
                        pltpu.VMEM((1, lanes), I32),
                        pltpu.SemaphoreType.DMA((sources,))],
        compiler_params=params(32),
        cost_estimate=cost(1, 1),
        name="add_rows",
    )(recv, neg_ids, own_neg)


def from_group(block, pairs, group):
    block = block[None]
    if group != 8:
        parts = lax.all_to_all(pairs, "dev", 0, 0, tiled=True)
        return [lax.all_gather(block, "dev", axis=0, tiled=True)], [parts]
    swap = lambda x, far: lax.ppermute(x, "dev", [(i, i ^ far) for i in range(group)])
    even = [block] + [swap(block, far) for far in (2, 4, 6)]
    parts = [pairs[0:1]] + [swap(pairs[n:n + 1], 2 * n) for n in (1, 2, 3)]
    even, parts = lax.optimization_barrier((even, parts))
    return [b for e in even for b in (e, swap(e, 1))], parts


def sum_pairs(parts, group):
    if group != 8:
        return parts.swapaxes(0, 1).reshape((group,) + parts.shape[2:])
    near = lax.ppermute(parts[1], "dev", [(i, i ^ 1) for i in range(group)])
    return (parts[0].astype(F32) + near.astype(F32)).astype(BF16)


def shift_layers(block, far, layers):
    return lax.ppermute(block, "grp", [(i, (i + far) % layers) for i in range(layers)])


def everywhere(values):
    for axis in ("dev", "grp"):
        count = lax.axis_size(axis)
        ring = [(i, (i + 1) % count) for i in range(count)]

        def turn(_, state):
            near = tuple(lax.ppermute(v, axis, ring) for v in state[0])
            return near, tuple(t + n for t, n in zip(state[1], near))

        values = lax.fori_loop(0, count - 1, turn, (values, values))[1]
    return values


def per_device(head_emb, tail_emb, relation, owners, owner_rows, entities, neg_rows, coef, bases):
    triples, cols = head_emb.shape
    group = lax.axis_size("dev")
    layers = lax.axis_size("grp")
    devices = layers * group
    neg_count = neg_rows.shape[1] * group
    ent_local = entities.shape[0]
    nrel, nb = coef.shape
    cap = 4 * triples // devices
    tall = LANES // cap * band(cols + 2, cap)
    share = pl.cdiv(cols, devices)
    step = LANES // math.gcd(group, LANES)
    span = pl.cdiv(pl.cdiv(nrel, devices), step) * step
    slots = 2 * triples // devices
    plan = (span, slots, slots - share)
    width = pl.cdiv(span + share, LANES) * LANES

    head_t, tail_t, owner_t, row_t = head_emb.T, tail_emb.T, owners.T, owner_rows.T
    coef_t, bases_t = coef.T, bases.T
    rel = relation.reshape(1, triples)

    sent_negs = pick_negs(neg_rows, entities.T, group)
    negs = lax.all_to_all(sent_negs, "dev", 0, 0, tiled=True)
    picked = pick_coef(rel, coef_t)
    coef_send, grads, rows, base, probs, hrel = score_step(
        rel, picked, negs, head_t, tail_t, row_t, bases_t, tall, neg_count, devices, plan, share)
    coef_recv = lax.all_to_all(coef_send, ("grp", "dev"), 0, 0, tiled=True)
    send = order_slots(grads, owner_t, devices, cap, cols + 2)
    send, coef_recv = lax.optimization_barrier((send, coef_recv))
    piece, flag = coef_sum(coef_recv, nb, plan, width)
    slabs = [piece] + [shift_layers(piece, far, layers) for far in range(1, layers)]
    me = lax.axis_index("dev").astype(I32).reshape(1)
    layer = lax.axis_index("grp").astype(I32).reshape(1)
    at = me if group == 8 else jnp.zeros((1,), I32)
    send, slabs = lax.optimization_barrier((send, slabs))
    recv = lax.all_to_all(send, ("grp", "dev"), 0, 0, tiled=True)
    pairs = sum_pairs(partial_step(at, probs, hrel, group, neg_count), group)
    pieces, parts = from_group(jnp.stack(slabs), pairs, group)
    own_neg = sum(part.astype(F32).sum(axis=0) for part in parts)
    pieces, own_neg = lax.optimization_barrier((pieces, own_neg))

    def packed():
        return tuple(spread(at, layer, pieces, span, share, nrel, cols))

    def dense():
        return everywhere((jnp.zeros((nb, nrel), F32).at[:, relation].add(rows), base.T))

    coef_grad, bases_grad = lax.cond(flag[0, 0] == 0, packed, dense)
    ent_grad = add_rows(recv, cap, cols, ent_local, neg_rows, own_neg)
    return ent_grad.T, coef_grad.T, bases_grad.T


def solution(mesh):
    return jax.shard_map(
        per_device,
        mesh=mesh,
        in_specs=(
            P(("grp", "dev"), None),
            P(("grp", "dev"), None),
            P(("grp", "dev")),
            P(("grp", "dev"), None),
            P(("grp", "dev"), None),
            P(("grp", "dev"), None),
            P(None, ("grp", "dev")),
            P(),
            P(),
        ),
        out_specs=(P(("grp", "dev"), None), P(), P()),
        check_vma=False,
    )
```

```python
import functools
import math

import jax
import jax.numpy as jnp
from jax import lax
from jax.experimental import pallas as pl
from jax.experimental.pallas import tpu as pltpu
from jax.sharding import PartitionSpec as P

F32, BF16, I32 = jnp.float32, jnp.bfloat16, jnp.int32
LANES = 128
PAD = 112


def nt(a, b, **kw):
    return lax.dot_general(a, b, (((1,), (1,)), ((), ())), preferred_element_type=F32, **kw)


def tn(a, b, **kw):
    return lax.dot_general(a, b, (((0,), (0,)), ((), ())), preferred_element_type=F32, **kw)


def nn(a, b, **kw):
    return lax.dot_general(a, b, (((1,), (0,)), ((), ())), preferred_element_type=F32, **kw)


def split(x):
    top = x.astype(BF16)
    return top, (x - top.astype(F32)).astype(BF16)


def padded(x):
    more = -x.shape[0] % 16
    return jnp.concatenate([x, jnp.zeros((more, x.shape[1]), x.dtype)], axis=0) if more else x


def precise(product, a, b):
    rows = a.shape[0]
    a = padded(a)
    tall = a.shape[0]
    a_top, a_low = split(a)
    b_top, b_low = split(b)
    both = product(jnp.concatenate([a_top, a_low], axis=0), b_top)
    return (both[0:tall] + both[tall:] + product(a_top, b_low))[0:rows]


def params(mib=56):
    return pltpu.CompilerParams(vmem_limit_bytes=mib * 1024 * 1024)


def cost(flops, nbytes):
    return pl.CostEstimate(flops=flops, bytes_accessed=nbytes, transcendentals=0)


def hits(ids, rows, first):
    row = lax.broadcasted_iota(I32, (rows, ids.shape[1]), 0)
    return jnp.where(row == ids - first, 1.0, 0.0).astype(BF16)


def pick_negs_kernel(ids_ref, ent_ref, out_ref, acc_ref):
    step = pl.program_id(0)
    width = ent_ref.shape[1]
    part = nn(ent_ref[...], hits(ids_ref[...], width, step * width))

    @pl.when(step == 0)
    def _():
        acc_ref[...] = part

    @pl.when(step > 0)
    def _():
        acc_ref[...] += part

    @pl.when(step == pl.num_programs(0) - 1)
    def _():
        rows = acc_ref[...].astype(BF16)
        for k in range(out_ref.shape[0]):
            out_ref[k] = rows


def pick_negs(ids, ent_t, group):
    cols, ent = ent_t.shape
    width = 2048
    return pl.pallas_call(
        pick_negs_kernel,
        grid=(ent // width,),
        in_specs=[
            pl.BlockSpec((1, ids.shape[1]), lambda i: (0, 0)),
            pl.BlockSpec((cols, width), lambda i: (0, i)),
        ],
        out_specs=pl.BlockSpec((group, cols, ids.shape[1]), lambda i: (0, 0, 0)),
        out_shape=jax.ShapeDtypeStruct((group, cols, ids.shape[1]), BF16),
        scratch_shapes=[pltpu.VMEM((cols, ids.shape[1]), F32)],
        compiler_params=params(),
        cost_estimate=cost(2 * cols * ent * 128, cols * ent * 2),
        name="pick_negs",
    )(ids, ent_t)


def up_to_here():
    rows = lax.broadcasted_iota(I32, (LANES, LANES), 0)
    cols = lax.broadcasted_iota(I32, (LANES, LANES), 1)
    return jnp.where(rows <= cols, 1.0, 0.0).astype(BF16)


def up_to_here():
    rows = lax.broadcasted_iota(I32, (LANES, LANES), 0)
    cols = lax.broadcasted_iota(I32, (LANES, LANES), 1)
    return jnp.where(rows <= cols, 1.0, 0.0).astype(BF16)


def band(rows, slots):
    bands = LANES // slots
    return rows if bands == 1 else pl.cdiv(pl.cdiv(rows, bands), 16) * 16


def pick_coef_kernel(nrel, fold, rel_ref, coef_ref, picked_ref, halves, acc):
    step = pl.program_id(0)
    nb, width = coef_ref.shape
    part = width // fold
    tall = acc.shape[0]
    half = tall // 2
    lane = lax.broadcasted_iota(I32, (nb, part), 1) + step * width
    spare = [jnp.zeros((half - nb, part), F32)] * (half > nb)
    for f in range(fold):
        block = coef_ref[:, f * part:(f + 1) * part]
        block = jnp.where(lane < nrel - f * part, block, 0.0)
        low = block - block.astype(BF16).astype(F32)
        both = jnp.concatenate([block, *spare, low, *spare], axis=0)
        halves[f * tall:(f + 1) * tall] = both.astype(BF16)
    here = rel_ref[...] - step * width
    where = here // part
    here = jnp.where((here >= 0) & (here < width), here - where * part, -1)
    found = nn(halves[...], hits(here, part, 0))
    total = jnp.where(where == 0, found[0:tall], 0.0)
    for f in range(1, fold):
        total = jnp.where(where == f, found[f * tall:(f + 1) * tall], total)

    @pl.when(step == 0)
    def _():
        acc[...] = total

    @pl.when(step > 0)
    def _():
        acc[...] += total

    @pl.when(step == pl.num_programs(0) - 1)
    def _():
        picked_ref[...] = acc[0:nb] + acc[half:half + nb]


def pick_coef(rel, coef_t):
    nb, nrel = coef_t.shape
    triples = rel.shape[1]
    fold = 2
    width = fold * 1920
    tall = 2 * (pl.cdiv(nb, 8) * 8)
    return pl.pallas_call(
        functools.partial(pick_coef_kernel, nrel, fold),
        grid=(pl.cdiv(nrel, width),),
        in_specs=[
            pl.BlockSpec((1, triples), lambda i: (0, 0)),
            pl.BlockSpec((nb, width), lambda i: (0, i)),
        ],
        out_specs=pl.BlockSpec((nb, triples), lambda i: (0, 0)),
        out_shape=jax.ShapeDtypeStruct((nb, triples), F32),
        scratch_shapes=[pltpu.VMEM((fold * tall, width // fold), BF16),
                        pltpu.VMEM((tall, triples), F32)],
        compiler_params=params(),
        cost_estimate=cost(2 * tall * nrel * triples, nb * nrel * 4),
        name="pick_coef",
    )(rel, coef_t)


def slot_of_relation(rel, devices, plan):
    span, slots, room = plan
    triples = rel.shape[1]
    number = lax.broadcasted_iota(I32, (devices, LANES), 0)
    later = lax.broadcasted_iota(I32, (LANES, triples), 1)
    row = lax.broadcasted_iota(I32, (LANES, triples), 0)
    seen = jnp.zeros((1, triples), F32)
    same = []
    for b in range(triples // LANES):
        down = jnp.broadcast_to(
            rel[:, b * LANES:(b + 1) * LANES].astype(F32), (LANES, LANES)).T[:, 0:1]
        equal = jnp.where(down.astype(I32) == rel, 1.0, 0.0)
        same.append(equal.astype(BF16))
        before = jnp.where(row + b * LANES < later, equal, 0.0)
        seen = seen + jnp.sum(before, axis=0, keepdims=True)
    first = jnp.where(seen == 0.0, 1.0, 0.0)
    summer = rel // span
    marks = []
    for b in range(triples // LANES):
        lanes = slice(b * LANES, (b + 1) * LANES)
        marks.append(jnp.where(number == summer[:, lanes], first[:, lanes], 0.0))
    sums = nn(jnp.concatenate(marks, axis=0).astype(BF16), up_to_here())
    carry = jnp.zeros((devices, 1), F32)
    lead = []
    for b, mark in enumerate(marks):
        part = sums[b * devices:(b + 1) * devices]
        lead.append(jnp.sum(mark * (part + carry - 1.0), axis=0, keepdims=True))
        carry = carry + part[:, LANES - 1:LANES]
    lead = jnp.minimum(jnp.concatenate(lead, axis=1), 255.0)
    lead = jnp.broadcast_to(lead, (16, triples)).astype(BF16)
    slot = nn(lead, jnp.concatenate(same, axis=0))[0:1].astype(I32)
    fits = slot < room
    place = jnp.where(fits, summer * slots + slot, -1)
    local = jnp.where(seen == 0.0, rel - summer * span, -1)
    over = jnp.max(jnp.where(fits, 0.0, 1.0), axis=1, keepdims=True)
    return place, local, over


def coef_blocks(rows, base, place, local, over, devices, plan, share):
    span, slots, room = plan
    nb = rows.shape[0]
    cols = base.shape[1]
    lanes = devices * slots

    def halves(block):
        spare = jnp.zeros((PAD - block.shape[0], block.shape[1]), F32)
        return jnp.concatenate(split(jnp.concatenate([block, spare], axis=0)), axis=0)

    high = local // 64
    pair = jnp.concatenate([high, local - high * 64], axis=0)
    pair = jnp.where(local >= 0, pair, 0).astype(F32)
    both = nt(halves(jnp.concatenate([rows, pair], axis=0)), hits(place, lanes, 0))
    column = lax.broadcasted_iota(I32, (1, cols), 1)
    owner = column // share
    spots = owner * slots + room + column - owner * share
    both = both + nt(halves(base), hits(spots, lanes, 0))
    row = lax.broadcasted_iota(I32, (PAD, lanes), 0)
    return jnp.where(row == nb + 2, over, both[0:PAD] + both[PAD:])


def score_kernel(neg_count, plan, share, rel_ref, picked_ref, negs_ref, head_ref, tail_ref,
                 row_ref, bases_ref, send_ref, grads_ref, rows_ref, base_ref, probs_ref, hrel_ref):
    group, cols, per = negs_ref.shape
    triples = head_ref.shape[1]
    devices, high, _ = send_ref.shape
    slots = plan[1]
    picked = picked_ref[...]
    vec = precise(nn, bases_ref[...], picked)
    head = head_ref[...].astype(F32)
    tail = tail_ref[...].astype(F32)
    head_vec = head * vec
    gate = jax.nn.sigmoid(-jnp.sum(head_vec * tail, axis=0, keepdims=True))
    head_rel = head_vec.astype(BF16)
    hrel_ref[...] = head_rel
    mix = jnp.zeros((cols, triples), F32)
    for first in range(0, group, 8):
        negs = jnp.concatenate([negs_ref[first + k] for k in range(8)], axis=1)
        probs = (0.5 * jnp.tanh(0.5 * tn(negs, head_rel)) + 0.5).astype(BF16)
        probs_ref[first * per:(first + 8) * per] = probs
        mix = mix + nn(negs, probs)
    rel_grad = -gate * head * tail + head * mix / neg_count
    rows = precise(nn, bases_ref[...].T, rel_grad)
    base = precise(nt, picked, rel_grad)
    rows_ref[...] = rows
    base_ref[...] = base
    place, local, over = slot_of_relation(rel_ref[...], devices, plan)
    both = coef_blocks(rows, base, place, local, over, devices, plan, share)
    bands = LANES // slots
    if bands * high > PAD:
        spare = jnp.zeros((bands * high - PAD, both.shape[1]), F32)
        both = jnp.concatenate([both, spare], axis=0)
    for o in range(devices):
        block = [both[b * high:(b + 1) * high, o * slots:(o + 1) * slots] for b in range(bands)]
        send_ref[o] = jnp.concatenate(block, axis=1).astype(BF16)
    grads_ref[0:cols, 0:triples] = (-gate * vec * tail + vec * mix / neg_count).astype(BF16)
    grads_ref[0:cols, triples:] = (-gate * head * vec).astype(BF16)
    for side in range(2):
        ids = row_ref[side:side + 1]
        lanes = slice(side * triples, (side + 1) * triples)
        upper = ids // 64
        pair = jnp.concatenate([upper, ids - upper * 64], axis=0).astype(F32)
        more = grads_ref.shape[0] - cols - 2
        if more:
            pair = jnp.concatenate([pair, jnp.zeros((more, triples), F32)], axis=0)
        grads_ref[cols:, lanes] = pair.astype(BF16)


def score_step(rel, picked, negs, head_t, tail_t, rows, bases_t, tall, neg_count, devices, plan,
               share):
    group, cols, per = negs.shape
    triples = head_t.shape[1]
    nb = bases_t.shape[1]
    high = pl.cdiv(PAD * plan[1], 8 * LANES) * 8
    outs = [((devices, high, LANES), BF16), ((tall, 2 * triples), BF16), ((nb, triples), F32),
            ((nb, cols), F32), ((group * per, triples), BF16), ((cols, triples), BF16)]
    return pl.pallas_call(
        functools.partial(score_kernel, neg_count, plan, share),
        out_shape=[jax.ShapeDtypeStruct(s, d) for s, d in outs],
        compiler_params=params(),
        cost_estimate=cost(2 * cols * triples * 2 * group * per, 16 << 20),
        name="score_step",
    )(rel, picked, negs, head_t, tail_t, rows, bases_t)


def order_kernel(devices, slots, grads_ref, owner_ref, send_ref, pos):
    owners, high, _ = send_ref.shape
    bands = LANES // slots
    step = pl.program_id(0)

    @pl.when(step == 0)
    def _():
        owner = owner_ref[...]
        triples = owner.shape[1]
        number = lax.broadcasted_iota(I32, (devices, LANES), 0)
        parts, marks = [], []
        for side in range(2):
            for b in range(triples // LANES):
                part = owner[side:side + 1, b * LANES:(b + 1) * LANES]
                parts.append(part)
                marks.append(jnp.where(number == part, 1.0, 0.0))
        sums = nn(jnp.concatenate(marks, axis=0).astype(BF16), up_to_here())
        carry = jnp.zeros((devices, 1), F32)
        for b, (part, mark) in enumerate(zip(parts, marks)):
            here = sums[b * devices:(b + 1) * devices]
            slot = jnp.sum(mark * (here + carry), axis=0, keepdims=True) - 1.0
            pos[:, b * LANES:(b + 1) * LANES] = part * slots + slot.astype(I32)
            carry = carry + here[:, LANES - 1:LANES]

    part = nt(grads_ref[...], hits(pos[...], owners * slots, step * owners * slots))
    part = part.astype(BF16)
    for o in range(owners):
        at = o * slots
        block = [part[b * high:(b + 1) * high, at:at + slots] for b in range(bands)]
        send_ref[o] = jnp.concatenate(block, axis=1)


def order_slots(grads, owner_t, devices, slots, rows):
    owners = 512 // slots
    high = band(rows, slots)
    whole = lambda shape: pl.BlockSpec(shape, lambda i: (0,) * len(shape))
    return pl.pallas_call(
        functools.partial(order_kernel, devices, slots),
        grid=(devices // owners,),
        in_specs=[whole(grads.shape), whole(owner_t.shape)],
        out_specs=pl.BlockSpec((owners, high, LANES), lambda i: (i, 0, 0)),
        out_shape=jax.ShapeDtypeStruct((devices, high, LANES), BF16),
        scratch_shapes=[pltpu.VMEM((1, grads.shape[1]), I32)],
        compiler_params=params(),
        cost_estimate=cost(rows * grads.shape[1] * devices * slots * 2, 4 << 20),
        name="order_slots",
    )(grads, owner_t)


def partial_kernel(neg_count, me_ref, probs_ref, hrel_ref, parts_ref, block):
    half, per = parts_ref.shape[1], parts_ref.shape[3]
    for first in range(0, 2 * half, 8):
        part = nt(hrel_ref[...], probs_ref[first * per:(first + 8) * per]) / neg_count
        block[...] = part
        for k in range(8):
            lane = pl.multiple_of((k ^ me_ref[0]) * per, per)
            parts_ref[k % 2, (first + k) // 2] = block[:, pl.ds(lane, per)].astype(BF16)


def partial_step(me, probs, hrel, group, neg_count):
    cols = hrel.shape[0]
    whole = lambda shape: pl.BlockSpec(shape, lambda i, me: (0,) * len(shape))
    shape = (2, group // 2, cols, LANES)
    return pl.pallas_call(
        functools.partial(partial_kernel, neg_count),
        grid_spec=pltpu.PrefetchScalarGridSpec(
            num_scalar_prefetch=1,
            grid=(1,),
            in_specs=[whole(probs.shape), whole(hrel.shape)],
            out_specs=whole(shape),
            scratch_shapes=[pltpu.VMEM((cols, 8 * LANES), F32)],
        ),
        out_shape=jax.ShapeDtypeStruct(shape, BF16),
        compiler_params=params(),
        cost_estimate=cost(1, 1),
        name="partial_step",
    )(me, probs, hrel)


def coef_sum_kernel(nb, plan, recv_ref, out_ref, flag_ref, left):
    span, slots, room = plan
    sources, high, _ = recv_ref.shape
    bands = LANES // slots
    for s in range(0, sources, bands):
        lanes = slice(s * slots, (s + bands) * slots)
        tall = []
        for b in range(bands):
            block = [recv_ref[s + k, :, b * slots:(b + 1) * slots] for k in range(bands)]
            tall.append(jnp.concatenate(block, axis=1).astype(F32))
        left[:, lanes] = jnp.concatenate(tall, axis=0)[0:PAD].astype(BF16)
    extra = left[PAD - 16:PAD].astype(F32)
    at = nb - (PAD - 16)
    ids = (extra[at:at + 1] * 64.0 + extra[at + 1:at + 2]).astype(I32)
    lane = lax.broadcasted_iota(I32, ids.shape, 1)
    lane = lane - lane // slots * slots
    ids = jnp.where(lane < room, ids, span + lane - room)
    total = nt(left[0:PAD], hits(ids, out_ref.shape[1], 0))
    out_ref[...] = total[0:nb].astype(BF16)
    over = jnp.max(extra[at + 2:at + 3], axis=1, keepdims=True)
    flag_ref[...] = jnp.broadcast_to(over, flag_ref.shape).astype(I32)


def coef_sum(recv, nb, plan, width):
    sources = recv.shape[0]
    slots = plan[1]
    return pl.pallas_call(
        functools.partial(coef_sum_kernel, nb, plan),
        out_shape=[jax.ShapeDtypeStruct((nb, width), BF16), jax.ShapeDtypeStruct((1, LANES), I32)],
        scratch_shapes=[pltpu.VMEM((PAD, sources * slots), BF16)],
        compiler_params=params(20),
        cost_estimate=cost(1, 1),
        name="coef_sum",
    )(recv)


def spread_kernel(span, share, place_ref, *refs):
    sets, (coef_ref, base_ref, pieces, strips) = refs[:-4], refs[-4:]
    step = pl.program_id(0)
    group, layers, nb, _ = pieces.shape

    @pl.when(step == 0)
    def _():
        number = 0
        for ref in sets:
            for s in range(ref.shape[0]):
                pieces[number ^ place_ref[0]] = ref[s]
                number += 1

    slab = lax.rem(place_ref[1] - step + layers, layers)
    row = [pieces[k, slab].astype(F32) for k in range(group)]
    coef_ref[...] = jnp.concatenate([r[:, 0:span] for r in row], axis=1)
    strip = jnp.concatenate([r[:, span:span + share] for r in row], axis=1)
    strips[step] = jnp.concatenate([strip, jnp.zeros((PAD - nb, strip.shape[1]), F32)], axis=0)

    @pl.when(step == layers - 1)
    def _():
        whole = jnp.concatenate([strips[g] for g in range(layers)], axis=1)
        base_ref[...] = whole[0:nb, 0:base_ref.shape[0]].T


def spread(me, layer, sets, span, share, nrel, cols):
    group = sum(s.shape[0] for s in sets)
    _, layers, nb, width = sets[0].shape
    whole = lambda shape: pl.BlockSpec(shape, lambda i, place: (0,) * len(shape))
    return pl.pallas_call(
        functools.partial(spread_kernel, span, share),
        grid_spec=pltpu.PrefetchScalarGridSpec(
            num_scalar_prefetch=1,
            grid=(layers,),
            in_specs=[whole(s.shape) for s in sets],
            out_specs=[
                pl.BlockSpec((nb, group * span), lambda i, place: (0, i)),
                whole((cols, nb)),
            ],
            scratch_shapes=[pltpu.VMEM((group, layers, nb, width), BF16),
                            pltpu.VMEM((layers, PAD, group * share), F32)],
        ),
        out_shape=[jax.ShapeDtypeStruct((nb, nrel), F32), jax.ShapeDtypeStruct((cols, nb), F32)],
        compiler_params=params(),
        cost_estimate=cost(1, 1),
        name="spread",
    )(jnp.concatenate([me, layer]), *sets)


def add_rows_kernel(slots, recv_ref, neg_ref, own_ref, out_ref, grads, ids, sems):
    step = pl.program_id(0)
    cols, width = out_ref.shape
    sources, high, _ = recv_ref.shape
    bands = LANES // slots
    lanes = sources * slots

    @pl.when(step == 0)
    def _():
        copies = []
        if bands == 1:
            for s in range(sources):
                to = grads.at[:, s * slots:(s + 1) * slots]
                copies.append(pltpu.make_async_copy(recv_ref.at[s], to, sems.at[s]))
        else:
            for s in range(0, sources, bands):
                at = slice(s * slots, (s + bands) * slots)
                for b in range(bands):
                    block = [recv_ref[s + k, :, b * slots:(b + 1) * slots] for k in range(bands)]
                    grads[b * high:(b + 1) * high, at] = jnp.concatenate(block, axis=1)
        for copy in copies:
            copy.start()
        top, low = split(own_ref[...])
        grads[0:cols, lanes:lanes + LANES] = top
        grads[0:cols, lanes + LANES:] = low
        ids[:, lanes:lanes + LANES] = neg_ref[...]
        ids[:, lanes + LANES:] = neg_ref[...]
        for copy in copies:
            copy.wait()
        pair = grads[cols:cols + 2, 0:lanes].astype(F32)
        ids[:, 0:lanes] = (pair[0:1] * 64.0 + pair[1:2]).astype(I32)

    out_ref[...] = nt(grads[0:cols], hits(ids[...], width, step * width))


def add_rows(recv, slots, cols, ent, neg_ids, own_neg):
    sources, high, _ = recv.shape
    bands = LANES // slots
    width = 1024
    lanes = sources * slots + 2 * LANES
    whole = lambda shape: pl.BlockSpec(shape, lambda i: (0,) * len(shape))
    there = pl.BlockSpec(memory_space=pl.ANY) if bands == 1 else whole(recv.shape)
    return pl.pallas_call(
        functools.partial(add_rows_kernel, slots),
        grid=(ent // width,),
        in_specs=[there, whole(neg_ids.shape), whole(own_neg.shape)],
        out_specs=pl.BlockSpec((cols, width), lambda i: (0, i)),
        out_shape=jax.ShapeDtypeStruct((cols, ent), F32),
        scratch_shapes=[pltpu.VMEM((bands * high, lanes), BF16),
                        pltpu.VMEM((1, lanes), I32),
                        pltpu.SemaphoreType.DMA((sources,))],
        compiler_params=params(32),
        cost_estimate=cost(1, 1),
        name="add_rows",
    )(recv, neg_ids, own_neg)


def from_group(block, pairs, group):
    block = block[None]
    if group != 8:
        parts = lax.all_to_all(pairs, "dev", 0, 0, tiled=True)
        return [lax.all_gather(block, "dev", axis=0, tiled=True)], [parts]
    swap = lambda x, far: lax.ppermute(x, "dev", [(i, i ^ far) for i in range(group)])
    even = [block] + [swap(block, far) for far in (2, 4, 6)]
    parts = [pairs[0:1]] + [swap(pairs[n:n + 1], 2 * n) for n in (1, 2, 3)]
    even, parts = lax.optimization_barrier((even, parts))
    return [b for e in even for b in (e, swap(e, 1))], parts


def sum_pairs(parts, group):
    if group != 8:
        return parts.swapaxes(0, 1).reshape((group,) + parts.shape[2:])
    near = lax.ppermute(parts[1], "dev", [(i, i ^ 1) for i in range(group)])
    return (parts[0].astype(F32) + near.astype(F32)).astype(BF16)


def shift_layers(block, far, layers):
    return lax.ppermute(block, "grp", [(i, (i + far) % layers) for i in range(layers)])


def everywhere(values):
    for axis in ("dev", "grp"):
        count = lax.axis_size(axis)
        assert count & (count - 1) == 0
        far = 1
        while far < count:
            swap = [(i, i ^ far) for i in range(count)]
            values = tuple(v + lax.ppermute(v, axis, swap) for v in values)
            far *= 2
    return values


def per_device(head_emb, tail_emb, relation, owners, owner_rows, entities, neg_rows, coef, bases):
    triples, cols = head_emb.shape
    group = lax.axis_size("dev")
    layers = lax.axis_size("grp")
    devices = layers * group
    neg_count = neg_rows.shape[1] * group
    ent_local = entities.shape[0]
    nrel, nb = coef.shape
    cap = 4 * triples // devices
    tall = LANES // cap * band(cols + 2, cap)
    share = pl.cdiv(cols, devices)
    step = LANES // math.gcd(group, LANES)
    span = pl.cdiv(pl.cdiv(nrel, devices), step) * step
    slots = 2 * triples // devices
    plan = (span, slots, slots - share)
    width = pl.cdiv(span + share, LANES) * LANES

    head_t, tail_t, owner_t, row_t = head_emb.T, tail_emb.T, owners.T, owner_rows.T
    coef_t, bases_t = coef.T, bases.T
    rel = relation.reshape(1, triples)

    sent_negs = pick_negs(neg_rows, entities.T, group)
    negs = lax.all_to_all(sent_negs, "dev", 0, 0, tiled=True)
    picked = pick_coef(rel, coef_t)
    coef_send, grads, rows, base, probs, hrel = score_step(
        rel, picked, negs, head_t, tail_t, row_t, bases_t, tall, neg_count, devices, plan, share)
    coef_recv = lax.all_to_all(coef_send, ("grp", "dev"), 0, 0, tiled=True)
    send = order_slots(grads, owner_t, devices, cap, cols + 2)
    send, coef_recv = lax.optimization_barrier((send, coef_recv))
    piece, flag = coef_sum(coef_recv, nb, plan, width)
    slabs = [piece] + [shift_layers(piece, far, layers) for far in range(1, layers)]
    me = lax.axis_index("dev").astype(I32).reshape(1)
    layer = lax.axis_index("grp").astype(I32).reshape(1)
    at = me if group == 8 else jnp.zeros((1,), I32)
    send, slabs = lax.optimization_barrier((send, slabs))
    recv = lax.all_to_all(send, ("grp", "dev"), 0, 0, tiled=True)
    pairs = sum_pairs(partial_step(at, probs, hrel, group, neg_count), group)
    pieces, parts = from_group(jnp.stack(slabs), pairs, group)
    own_neg = sum(part.astype(F32).sum(axis=0) for part in parts)
    pieces, own_neg = lax.optimization_barrier((pieces, own_neg))

    def packed():
        return tuple(spread(at, layer, pieces, span, share, nrel, cols))

    def dense():
        return everywhere((jnp.zeros((nb, nrel), F32).at[:, relation].add(rows), base.T))

    coef_grad, bases_grad = lax.cond(flag[0, 0] == 0, packed, dense)
    ent_grad = add_rows(recv, cap, cols, ent_local, neg_rows, own_neg)
    return ent_grad.T, coef_grad.T, bases_grad.T


def solution(mesh):
    return jax.shard_map(
        per_device,
        mesh=mesh,
        in_specs=(
            P(("grp", "dev"), None),
            P(("grp", "dev"), None),
            P(("grp", "dev")),
            P(("grp", "dev"), None),
            P(("grp", "dev"), None),
            P(("grp", "dev"), None),
            P(None, ("grp", "dev")),
            P(),
            P(),
        ),
        out_specs=(P(("grp", "dev"), None), P(), P()),
        check_vma=False,
    )
```

```python
import functools
import math

import jax
import jax.numpy as jnp
from jax import lax
from jax.experimental import pallas as pl
from jax.experimental.pallas import tpu as pltpu
from jax.sharding import PartitionSpec as P

F32, BF16, I32 = jnp.float32, jnp.bfloat16, jnp.int32
LANES = 128
PAD = 112


def nt(a, b, **kw):
    return lax.dot_general(a, b, (((1,), (1,)), ((), ())), preferred_element_type=F32, **kw)


def tn(a, b, **kw):
    return lax.dot_general(a, b, (((0,), (0,)), ((), ())), preferred_element_type=F32, **kw)


def nn(a, b, **kw):
    return lax.dot_general(a, b, (((1,), (0,)), ((), ())), preferred_element_type=F32, **kw)


def split(x):
    top = x.astype(BF16)
    return top, (x - top.astype(F32)).astype(BF16)


def padded(x):
    more = -x.shape[0] % 16
    return jnp.concatenate([x, jnp.zeros((more, x.shape[1]), x.dtype)], axis=0) if more else x


def precise(product, a, b):
    rows = a.shape[0]
    a = padded(a)
    tall = a.shape[0]
    a_top, a_low = split(a)
    b_top, b_low = split(b)
    both = product(jnp.concatenate([a_top, a_low], axis=0), b_top)
    return (both[0:tall] + both[tall:] + product(a_top, b_low))[0:rows]


def params(mib=56):
    return pltpu.CompilerParams(vmem_limit_bytes=mib * 1024 * 1024)


def cost(flops, nbytes):
    return pl.CostEstimate(flops=flops, bytes_accessed=nbytes, transcendentals=0)


def hits(ids, rows, first):
    row = lax.broadcasted_iota(I32, (rows, ids.shape[1]), 0)
    return jnp.where(row == ids - first, 1.0, 0.0).astype(BF16)


def pick_negs_kernel(ids_ref, ent_ref, out_ref, acc_ref):
    step = pl.program_id(0)
    width = ent_ref.shape[1]
    part = nn(ent_ref[...], hits(ids_ref[...], width, step * width))

    @pl.when(step == 0)
    def _():
        acc_ref[...] = part

    @pl.when(step > 0)
    def _():
        acc_ref[...] += part

    @pl.when(step == pl.num_programs(0) - 1)
    def _():
        rows = acc_ref[...].astype(BF16)
        for k in range(out_ref.shape[0]):
            out_ref[k] = rows


def pick_negs(ids, ent_t, group):
    cols, ent = ent_t.shape
    width = 2048
    return pl.pallas_call(
        pick_negs_kernel,
        grid=(ent // width,),
        in_specs=[
            pl.BlockSpec((1, ids.shape[1]), lambda i: (0, 0)),
            pl.BlockSpec((cols, width), lambda i: (0, i)),
        ],
        out_specs=pl.BlockSpec((group, cols, ids.shape[1]), lambda i: (0, 0, 0)),
        out_shape=jax.ShapeDtypeStruct((group, cols, ids.shape[1]), BF16),
        scratch_shapes=[pltpu.VMEM((cols, ids.shape[1]), F32)],
        compiler_params=params(),
        cost_estimate=cost(2 * cols * ent * 128, cols * ent * 2),
        name="pick_negs",
    )(ids, ent_t)


def up_to_here():
    rows = lax.broadcasted_iota(I32, (LANES, LANES), 0)
    cols = lax.broadcasted_iota(I32, (LANES, LANES), 1)
    return jnp.where(rows <= cols, 1.0, 0.0).astype(BF16)


def up_to_here():
    rows = lax.broadcasted_iota(I32, (LANES, LANES), 0)
    cols = lax.broadcasted_iota(I32, (LANES, LANES), 1)
    return jnp.where(rows <= cols, 1.0, 0.0).astype(BF16)


def band(rows, slots):
    bands = LANES // slots
    return rows if bands == 1 else pl.cdiv(pl.cdiv(rows, bands), 16) * 16


def pick_coef_kernel(nrel, fold, rel_ref, coef_ref, picked_ref, halves, acc):
    step = pl.program_id(0)
    nb, width = coef_ref.shape
    part = width // fold
    tall = acc.shape[0]
    half = tall // 2
    lane = lax.broadcasted_iota(I32, (nb, part), 1) + step * width
    spare = [jnp.zeros((half - nb, part), F32)] * (half > nb)
    for f in range(fold):
        block = coef_ref[:, f * part:(f + 1) * part]
        block = jnp.where(lane < nrel - f * part, block, 0.0)
        low = block - block.astype(BF16).astype(F32)
        both = jnp.concatenate([block, *spare, low, *spare], axis=0)
        halves[f * tall:(f + 1) * tall] = both.astype(BF16)
    here = rel_ref[...] - step * width
    where = here // part
    here = jnp.where((here >= 0) & (here < width), here - where * part, -1)
    found = nn(halves[...], hits(here, part, 0))
    total = jnp.where(where == 0, found[0:tall], 0.0)
    for f in range(1, fold):
        total = jnp.where(where == f, found[f * tall:(f + 1) * tall], total)

    @pl.when(step == 0)
    def _():
        acc[...] = total

    @pl.when(step > 0)
    def _():
        acc[...] += total

    @pl.when(step == pl.num_programs(0) - 1)
    def _():
        picked_ref[...] = acc[0:nb] + acc[half:half + nb]


def pick_coef(rel, coef_t):
    nb, nrel = coef_t.shape
    triples = rel.shape[1]
    fold = 2
    width = fold * 1920
    tall = 2 * (pl.cdiv(nb, 8) * 8)
    return pl.pallas_call(
        functools.partial(pick_coef_kernel, nrel, fold),
        grid=(pl.cdiv(nrel, width),),
        in_specs=[
            pl.BlockSpec((1, triples), lambda i: (0, 0)),
            pl.BlockSpec((nb, width), lambda i: (0, i)),
        ],
        out_specs=pl.BlockSpec((nb, triples), lambda i: (0, 0)),
        out_shape=jax.ShapeDtypeStruct((nb, triples), F32),
        scratch_shapes=[pltpu.VMEM((fold * tall, width // fold), BF16),
                        pltpu.VMEM((tall, triples), F32)],
        compiler_params=params(),
        cost_estimate=cost(2 * tall * nrel * triples, nb * nrel * 4),
        name="pick_coef",
    )(rel, coef_t)


def slot_of_relation(rel, devices, plan):
    span, slots, room = plan
    triples = rel.shape[1]
    number = lax.broadcasted_iota(I32, (devices, LANES), 0)
    later = lax.broadcasted_iota(I32, (LANES, triples), 1)
    row = lax.broadcasted_iota(I32, (LANES, triples), 0)
    seen = jnp.zeros((1, triples), F32)
    same = []
    for b in range(triples // LANES):
        down = jnp.broadcast_to(
            rel[:, b * LANES:(b + 1) * LANES].astype(F32), (LANES, LANES)).T[:, 0:1]
        equal = jnp.where(down.astype(I32) == rel, 1.0, 0.0)
        same.append(equal.astype(BF16))
        before = jnp.where(row + b * LANES < later, equal, 0.0)
        seen = seen + jnp.sum(before, axis=0, keepdims=True)
    first = jnp.where(seen == 0.0, 1.0, 0.0)
    summer = rel // span
    marks = []
    for b in range(triples // LANES):
        lanes = slice(b * LANES, (b + 1) * LANES)
        marks.append(jnp.where(number == summer[:, lanes], first[:, lanes], 0.0))
    sums = nn(jnp.concatenate(marks, axis=0).astype(BF16), up_to_here())
    carry = jnp.zeros((devices, 1), F32)
    lead = []
    for b, mark in enumerate(marks):
        part = sums[b * devices:(b + 1) * devices]
        lead.append(jnp.sum(mark * (part + carry - 1.0), axis=0, keepdims=True))
        carry = carry + part[:, LANES - 1:LANES]
    lead = jnp.minimum(jnp.concatenate(lead, axis=1), 255.0)
    lead = jnp.broadcast_to(lead, (16, triples)).astype(BF16)
    slot = nn(lead, jnp.concatenate(same, axis=0))[0:1].astype(I32)
    fits = slot < room
    place = jnp.where(fits, summer * slots + slot, -1)
    local = jnp.where(seen == 0.0, rel - summer * span, -1)
    over = jnp.max(jnp.where(fits, 0.0, 1.0), axis=1, keepdims=True)
    return place, local, over


def coef_blocks(rows, base, place, local, over, devices, plan, share):
    span, slots, room = plan
    nb = rows.shape[0]
    cols = base.shape[1]
    lanes = devices * slots

    high = local // 64
    pair = jnp.concatenate([high, local - high * 64], axis=0)
    pair = jnp.where(local >= 0, pair, 0).astype(F32)
    tall = pl.cdiv(nb + 3, 8) * 8
    left = jnp.concatenate([rows, pair, jnp.zeros((tall - nb - 2, rows.shape[1]), F32)], axis=0)
    right = jnp.concatenate([base, jnp.zeros((tall - nb, cols), F32)], axis=0)
    both = jnp.concatenate([left, right], axis=1)
    low = both - both.astype(BF16).astype(F32)
    column = lax.broadcasted_iota(I32, (1, cols), 1)
    owner = column // share
    spots = owner * slots + room + column - owner * share
    spots = jnp.concatenate([place, spots], axis=1)
    both = nt(jnp.concatenate([both, low], axis=0).astype(BF16), hits(spots, lanes, 0))
    row = lax.broadcasted_iota(I32, (tall, lanes), 0)
    both = jnp.where(row == nb + 2, over, both[0:tall] + both[tall:])
    return jnp.concatenate([both, jnp.zeros((PAD - tall, lanes), F32)], axis=0)


def score_kernel(neg_count, plan, share, rel_ref, picked_ref, negs_ref, head_ref, tail_ref,
                 row_ref, bases_ref, send_ref, grads_ref, rows_ref, base_ref, probs_ref, hrel_ref):
    group, cols, per = negs_ref.shape
    triples = head_ref.shape[1]
    devices, high, _ = send_ref.shape
    slots = plan[1]
    picked = picked_ref[...]
    vec = precise(nn, bases_ref[...], picked)
    head = head_ref[...].astype(F32)
    tail = tail_ref[...].astype(F32)
    head_vec = head * vec
    gate = jax.nn.sigmoid(-jnp.sum(head_vec * tail, axis=0, keepdims=True))
    head_rel = head_vec.astype(BF16)
    hrel_ref[...] = head_rel
    mix = jnp.zeros((cols, triples), F32)
    for first in range(0, group, 8):
        negs = jnp.concatenate([negs_ref[first + k] for k in range(8)], axis=1)
        probs = (0.5 * jnp.tanh(0.5 * tn(negs, head_rel)) + 0.5).astype(BF16)
        probs_ref[first * per:(first + 8) * per] = probs
        mix = mix + nn(negs, probs)
    rel_grad = -gate * head * tail + head * mix / neg_count
    rows = precise(nn, bases_ref[...].T, rel_grad)
    base = precise(nt, picked, rel_grad)
    rows_ref[...] = rows
    base_ref[...] = base
    place, local, over = slot_of_relation(rel_ref[...], devices, plan)
    both = coef_blocks(rows, base, place, local, over, devices, plan, share)
    bands = LANES // slots
    if bands * high > PAD:
        spare = jnp.zeros((bands * high - PAD, both.shape[1]), F32)
        both = jnp.concatenate([both, spare], axis=0)
    for o in range(devices):
        block = [both[b * high:(b + 1) * high, o * slots:(o + 1) * slots] for b in range(bands)]
        send_ref[o] = jnp.concatenate(block, axis=1).astype(BF16)
    grads_ref[0:cols, 0:triples] = (-gate * vec * tail + vec * mix / neg_count).astype(BF16)
    grads_ref[0:cols, triples:] = (-gate * head * vec).astype(BF16)
    for side in range(2):
        ids = row_ref[side:side + 1]
        lanes = slice(side * triples, (side + 1) * triples)
        upper = ids // 64
        pair = jnp.concatenate([upper, ids - upper * 64], axis=0).astype(F32)
        more = grads_ref.shape[0] - cols - 2
        if more:
            pair = jnp.concatenate([pair, jnp.zeros((more, triples), F32)], axis=0)
        grads_ref[cols:, lanes] = pair.astype(BF16)


def score_step(rel, picked, negs, head_t, tail_t, rows, bases_t, tall, neg_count, devices, plan,
               share):
    group, cols, per = negs.shape
    triples = head_t.shape[1]
    nb = bases_t.shape[1]
    high = pl.cdiv(PAD * plan[1], 8 * LANES) * 8
    outs = [((devices, high, LANES), BF16), ((tall, 2 * triples), BF16), ((nb, triples), F32),
            ((nb, cols), F32), ((group * per, triples), BF16), ((cols, triples), BF16)]
    return pl.pallas_call(
        functools.partial(score_kernel, neg_count, plan, share),
        out_shape=[jax.ShapeDtypeStruct(s, d) for s, d in outs],
        compiler_params=params(),
        cost_estimate=cost(2 * cols * triples * 2 * group * per, 16 << 20),
        name="score_step",
    )(rel, picked, negs, head_t, tail_t, rows, bases_t)


def order_kernel(devices, slots, grads_ref, owner_ref, send_ref, pos):
    owners, high, _ = send_ref.shape
    bands = LANES // slots
    step = pl.program_id(0)

    @pl.when(step == 0)
    def _():
        owner = owner_ref[...]
        triples = owner.shape[1]
        number = lax.broadcasted_iota(I32, (devices, LANES), 0)
        parts, marks = [], []
        for side in range(2):
            for b in range(triples // LANES):
                part = owner[side:side + 1, b * LANES:(b + 1) * LANES]
                parts.append(part)
                marks.append(jnp.where(number == part, 1.0, 0.0))
        sums = nn(jnp.concatenate(marks, axis=0).astype(BF16), up_to_here())
        carry = jnp.zeros((devices, 1), F32)
        for b, (part, mark) in enumerate(zip(parts, marks)):
            here = sums[b * devices:(b + 1) * devices]
            slot = jnp.sum(mark * (here + carry), axis=0, keepdims=True) - 1.0
            pos[:, b * LANES:(b + 1) * LANES] = part * slots + slot.astype(I32)
            carry = carry + here[:, LANES - 1:LANES]

    part = nt(grads_ref[...], hits(pos[...], owners * slots, step * owners * slots))
    part = part.astype(BF16)
    for o in range(owners):
        at = o * slots
        block = [part[b * high:(b + 1) * high, at:at + slots] for b in range(bands)]
        send_ref[o] = jnp.concatenate(block, axis=1)


def order_slots(grads, owner_t, devices, slots, rows):
    owners = 512 // slots
    high = band(rows, slots)
    whole = lambda shape: pl.BlockSpec(shape, lambda i: (0,) * len(shape))
    return pl.pallas_call(
        functools.partial(order_kernel, devices, slots),
        grid=(devices // owners,),
        in_specs=[whole(grads.shape), whole(owner_t.shape)],
        out_specs=pl.BlockSpec((owners, high, LANES), lambda i: (i, 0, 0)),
        out_shape=jax.ShapeDtypeStruct((devices, high, LANES), BF16),
        scratch_shapes=[pltpu.VMEM((1, grads.shape[1]), I32)],
        compiler_params=params(),
        cost_estimate=cost(rows * grads.shape[1] * devices * slots * 2, 4 << 20),
        name="order_slots",
    )(grads, owner_t)


def partial_kernel(neg_count, me_ref, probs_ref, hrel_ref, parts_ref, block):
    half, per = parts_ref.shape[1], parts_ref.shape[3]
    for first in range(0, 2 * half, 8):
        part = nt(hrel_ref[...], probs_ref[first * per:(first + 8) * per]) / neg_count
        block[...] = part
        for k in range(8):
            lane = pl.multiple_of((k ^ me_ref[0]) * per, per)
            parts_ref[k % 2, (first + k) // 2] = block[:, pl.ds(lane, per)].astype(BF16)


def partial_step(me, probs, hrel, group, neg_count):
    cols = hrel.shape[0]
    whole = lambda shape: pl.BlockSpec(shape, lambda i, me: (0,) * len(shape))
    shape = (2, group // 2, cols, LANES)
    return pl.pallas_call(
        functools.partial(partial_kernel, neg_count),
        grid_spec=pltpu.PrefetchScalarGridSpec(
            num_scalar_prefetch=1,
            grid=(1,),
            in_specs=[whole(probs.shape), whole(hrel.shape)],
            out_specs=whole(shape),
            scratch_shapes=[pltpu.VMEM((cols, 8 * LANES), F32)],
        ),
        out_shape=jax.ShapeDtypeStruct(shape, BF16),
        compiler_params=params(),
        cost_estimate=cost(1, 1),
        name="partial_step",
    )(me, probs, hrel)


def coef_sum_kernel(nb, plan, recv_ref, out_ref, flag_ref, left):
    span, slots, room = plan
    sources, high, _ = recv_ref.shape
    bands = LANES // slots
    for s in range(0, sources, bands):
        lanes = slice(s * slots, (s + bands) * slots)
        tall = []
        for b in range(bands):
            block = [recv_ref[s + k, :, b * slots:(b + 1) * slots] for k in range(bands)]
            tall.append(jnp.concatenate(block, axis=1).astype(F32))
        left[:, lanes] = jnp.concatenate(tall, axis=0)[0:PAD].astype(BF16)
    extra = left[PAD - 16:PAD].astype(F32)
    at = nb - (PAD - 16)
    ids = (extra[at:at + 1] * 64.0 + extra[at + 1:at + 2]).astype(I32)
    lane = lax.broadcasted_iota(I32, ids.shape, 1)
    lane = lane - lane // slots * slots
    ids = jnp.where(lane < room, ids, span + lane - room)
    total = nt(left[0:PAD], hits(ids, out_ref.shape[1], 0))
    out_ref[...] = total[0:nb].astype(BF16)
    over = jnp.max(extra[at + 2:at + 3], axis=1, keepdims=True)
    flag_ref[...] = jnp.broadcast_to(over, flag_ref.shape).astype(I32)


def coef_sum(recv, nb, plan, width):
    sources = recv.shape[0]
    slots = plan[1]
    return pl.pallas_call(
        functools.partial(coef_sum_kernel, nb, plan),
        out_shape=[jax.ShapeDtypeStruct((nb, width), BF16), jax.ShapeDtypeStruct((1, LANES), I32)],
        scratch_shapes=[pltpu.VMEM((PAD, sources * slots), BF16)],
        compiler_params=params(20),
        cost_estimate=cost(1, 1),
        name="coef_sum",
    )(recv)


def spread_kernel(span, share, place_ref, *refs):
    sets, (coef_ref, base_ref, pieces, strips) = refs[:-4], refs[-4:]
    step = pl.program_id(0)
    group, layers, nb, _ = pieces.shape

    @pl.when(step == 0)
    def _():
        number = 0
        for ref in sets:
            for s in range(ref.shape[0]):
                pieces[number ^ place_ref[0]] = ref[s]
                number += 1

    slab = lax.rem(place_ref[1] - step + layers, layers)
    row = [pieces[k, slab].astype(F32) for k in range(group)]
    coef_ref[...] = jnp.concatenate([r[:, 0:span] for r in row], axis=1)
    strip = jnp.concatenate([r[:, span:span + share] for r in row], axis=1)
    strips[step] = jnp.concatenate([strip, jnp.zeros((PAD - nb, strip.shape[1]), F32)], axis=0)

    @pl.when(step == layers - 1)
    def _():
        whole = jnp.concatenate([strips[g] for g in range(layers)], axis=1)
        base_ref[...] = whole[0:nb, 0:base_ref.shape[0]].T


def spread(me, layer, sets, span, share, nrel, cols):
    group = sum(s.shape[0] for s in sets)
    _, layers, nb, width = sets[0].shape
    whole = lambda shape: pl.BlockSpec(shape, lambda i, place: (0,) * len(shape))
    return pl.pallas_call(
        functools.partial(spread_kernel, span, share),
        grid_spec=pltpu.PrefetchScalarGridSpec(
            num_scalar_prefetch=1,
            grid=(layers,),
            in_specs=[whole(s.shape) for s in sets],
            out_specs=[
                pl.BlockSpec((nb, group * span), lambda i, place: (0, i)),
                whole((cols, nb)),
            ],
            scratch_shapes=[pltpu.VMEM((group, layers, nb, width), BF16),
                            pltpu.VMEM((layers, PAD, group * share), F32)],
        ),
        out_shape=[jax.ShapeDtypeStruct((nb, nrel), F32), jax.ShapeDtypeStruct((cols, nb), F32)],
        compiler_params=params(),
        cost_estimate=cost(1, 1),
        name="spread",
    )(jnp.concatenate([me, layer]), *sets)


def add_rows_kernel(slots, recv_ref, neg_ref, own_ref, out_ref, grads, ids, sems):
    step = pl.program_id(0)
    cols, width = out_ref.shape
    sources, high, _ = recv_ref.shape
    bands = LANES // slots
    lanes = sources * slots

    @pl.when(step == 0)
    def _():
        copies = []
        if bands == 1:
            for s in range(sources):
                to = grads.at[:, s * slots:(s + 1) * slots]
                copies.append(pltpu.make_async_copy(recv_ref.at[s], to, sems.at[s]))
        else:
            for s in range(0, sources, bands):
                at = slice(s * slots, (s + bands) * slots)
                for b in range(bands):
                    block = [recv_ref[s + k, :, b * slots:(b + 1) * slots] for k in range(bands)]
                    grads[b * high:(b + 1) * high, at] = jnp.concatenate(block, axis=1)
        for copy in copies:
            copy.start()
        top, low = split(own_ref[...])
        grads[0:cols, lanes:lanes + LANES] = top
        grads[0:cols, lanes + LANES:] = low
        ids[:, lanes:lanes + LANES] = neg_ref[...]
        ids[:, lanes + LANES:] = neg_ref[...]
        for copy in copies:
            copy.wait()
        pair = grads[cols:cols + 2, 0:lanes].astype(F32)
        ids[:, 0:lanes] = (pair[0:1] * 64.0 + pair[1:2]).astype(I32)

    out_ref[...] = nt(grads[0:cols], hits(ids[...], width, step * width))


def add_rows(recv, slots, cols, ent, neg_ids, own_neg):
    sources, high, _ = recv.shape
    bands = LANES // slots
    width = 1024
    lanes = sources * slots + 2 * LANES
    whole = lambda shape: pl.BlockSpec(shape, lambda i: (0,) * len(shape))
    there = pl.BlockSpec(memory_space=pl.ANY) if bands == 1 else whole(recv.shape)
    return pl.pallas_call(
        functools.partial(add_rows_kernel, slots),
        grid=(ent // width,),
        in_specs=[there, whole(neg_ids.shape), whole(own_neg.shape)],
        out_specs=pl.BlockSpec((cols, width), lambda i: (0, i)),
        out_shape=jax.ShapeDtypeStruct((cols, ent), F32),
        scratch_shapes=[pltpu.VMEM((bands * high, lanes), BF16),
                        pltpu.VMEM((1, lanes), I32),
                        pltpu.SemaphoreType.DMA((sources,))],
        compiler_params=params(32),
        cost_estimate=cost(1, 1),
        name="add_rows",
    )(recv, neg_ids, own_neg)


def from_group(block, pairs, group):
    block = block[None]
    if group != 8:
        parts = lax.all_to_all(pairs, "dev", 0, 0, tiled=True)
        return [lax.all_gather(block, "dev", axis=0, tiled=True)], [parts]
    swap = lambda x, far: lax.ppermute(x, "dev", [(i, i ^ far) for i in range(group)])
    even = [block] + [swap(block, far) for far in (2, 4, 6)]
    parts = [pairs[0:1]] + [swap(pairs[n:n + 1], 2 * n) for n in (1, 2, 3)]
    even, parts = lax.optimization_barrier((even, parts))
    return [b for e in even for b in (e, swap(e, 1))], parts


def sum_pairs(parts, group):
    if group != 8:
        return parts.swapaxes(0, 1).reshape((group,) + parts.shape[2:])
    near = lax.ppermute(parts[1], "dev", [(i, i ^ 1) for i in range(group)])
    return (parts[0].astype(F32) + near.astype(F32)).astype(BF16)


def shift_layers(block, far, layers):
    return lax.ppermute(block, "grp", [(i, (i + far) % layers) for i in range(layers)])


def everywhere(values):
    for axis in ("dev", "grp"):
        count = lax.axis_size(axis)
        assert count & (count - 1) == 0
        far = 1
        while far < count:
            swap = [(i, i ^ far) for i in range(count)]
            values = tuple(v + lax.ppermute(v, axis, swap) for v in values)
            far *= 2
    return values


def per_device(head_emb, tail_emb, relation, owners, owner_rows, entities, neg_rows, coef, bases):
    triples, cols = head_emb.shape
    group = lax.axis_size("dev")
    layers = lax.axis_size("grp")
    devices = layers * group
    neg_count = neg_rows.shape[1] * group
    ent_local = entities.shape[0]
    nrel, nb = coef.shape
    cap = 4 * triples // devices
    tall = LANES // cap * band(cols + 2, cap)
    share = pl.cdiv(cols, devices)
    step = LANES // math.gcd(group, LANES)
    span = pl.cdiv(pl.cdiv(nrel, devices), step) * step
    slots = 2 * triples // devices
    plan = (span, slots, slots - share)
    width = pl.cdiv(span + share, LANES) * LANES

    head_t, tail_t, owner_t, row_t = head_emb.T, tail_emb.T, owners.T, owner_rows.T
    coef_t, bases_t = coef.T, bases.T
    rel = relation.reshape(1, triples)

    sent_negs = pick_negs(neg_rows, entities.T, group)
    negs = lax.all_to_all(sent_negs, "dev", 0, 0, tiled=True)
    picked = pick_coef(rel, coef_t)
    coef_send, grads, rows, base, probs, hrel = score_step(
        rel, picked, negs, head_t, tail_t, row_t, bases_t, tall, neg_count, devices, plan, share)
    coef_recv = lax.all_to_all(coef_send, ("grp", "dev"), 0, 0, tiled=True)
    send = order_slots(grads, owner_t, devices, cap, cols + 2)
    send, coef_recv = lax.optimization_barrier((send, coef_recv))
    piece, flag = coef_sum(coef_recv, nb, plan, width)
    slabs = [piece] + [shift_layers(piece, far, layers) for far in range(1, layers)]
    me = lax.axis_index("dev").astype(I32).reshape(1)
    layer = lax.axis_index("grp").astype(I32).reshape(1)
    at = me if group == 8 else jnp.zeros((1,), I32)
    send, slabs = lax.optimization_barrier((send, slabs))
    recv = lax.all_to_all(send, ("grp", "dev"), 0, 0, tiled=True)
    pairs = sum_pairs(partial_step(at, probs, hrel, group, neg_count), group)
    pieces, parts = from_group(jnp.stack(slabs), pairs, group)
    own_neg = sum(part.astype(F32).sum(axis=0) for part in parts)
    pieces, own_neg = lax.optimization_barrier((pieces, own_neg))

    def packed():
        return tuple(spread(at, layer, pieces, span, share, nrel, cols))

    def dense():
        return everywhere((jnp.zeros((nb, nrel), F32).at[:, relation].add(rows), base.T))

    coef_grad, bases_grad = lax.cond(flag[0, 0] == 0, packed, dense)
    ent_grad = add_rows(recv, cap, cols, ent_local, neg_rows, own_neg)
    return ent_grad.T, coef_grad.T, bases_grad.T


def solution(mesh):
    return jax.shard_map(
        per_device,
        mesh=mesh,
        in_specs=(
            P(("grp", "dev"), None),
            P(("grp", "dev"), None),
            P(("grp", "dev")),
            P(("grp", "dev"), None),
            P(("grp", "dev"), None),
            P(("grp", "dev"), None),
            P(None, ("grp", "dev")),
            P(),
            P(),
        ),
        out_specs=(P(("grp", "dev"), None), P(), P()),
        check_vma=False,
    )
```

```python
import functools
import math

import jax
import jax.numpy as jnp
from jax import lax
from jax.experimental import pallas as pl
from jax.experimental.pallas import tpu as pltpu
from jax.sharding import PartitionSpec as P

F32, BF16, I32 = jnp.float32, jnp.bfloat16, jnp.int32
LANES = 128
PAD = 112


def nt(a, b, **kw):
    return lax.dot_general(a, b, (((1,), (1,)), ((), ())), preferred_element_type=F32, **kw)


def tn(a, b, **kw):
    return lax.dot_general(a, b, (((0,), (0,)), ((), ())), preferred_element_type=F32, **kw)


def nn(a, b, **kw):
    return lax.dot_general(a, b, (((1,), (0,)), ((), ())), preferred_element_type=F32, **kw)


def split(x):
    top = x.astype(BF16)
    return top, (x - top.astype(F32)).astype(BF16)


def padded(x):
    more = -x.shape[0] % 16
    return jnp.concatenate([x, jnp.zeros((more, x.shape[1]), x.dtype)], axis=0) if more else x


def precise(product, a, b):
    rows = a.shape[0]
    a = padded(a)
    tall = a.shape[0]
    a_top, a_low = split(a)
    b_top, b_low = split(b)
    both = product(jnp.concatenate([a_top, a_low], axis=0), b_top)
    return (both[0:tall] + both[tall:] + product(a_top, b_low))[0:rows]


def params(mib=56):
    return pltpu.CompilerParams(vmem_limit_bytes=mib * 1024 * 1024)


def cost(flops, nbytes):
    return pl.CostEstimate(flops=flops, bytes_accessed=nbytes, transcendentals=0)


def hits(ids, rows, first):
    row = lax.broadcasted_iota(I32, (rows, ids.shape[1]), 0)
    return jnp.where(row == ids - first, 1.0, 0.0).astype(BF16)


def pick_negs_kernel(ids_ref, ent_ref, out_ref, acc_ref):
    step = pl.program_id(0)
    width = ent_ref.shape[1]
    part = nn(ent_ref[...], hits(ids_ref[...], width, step * width))

    @pl.when(step == 0)
    def _():
        acc_ref[...] = part

    @pl.when(step > 0)
    def _():
        acc_ref[...] += part

    @pl.when(step == pl.num_programs(0) - 1)
    def _():
        rows = acc_ref[...].astype(BF16)
        for k in range(out_ref.shape[0]):
            out_ref[k] = rows


def pick_negs(ids, ent_t, group):
    cols, ent = ent_t.shape
    width = 2048
    return pl.pallas_call(
        pick_negs_kernel,
        grid=(ent // width,),
        in_specs=[
            pl.BlockSpec((1, ids.shape[1]), lambda i: (0, 0)),
            pl.BlockSpec((cols, width), lambda i: (0, i)),
        ],
        out_specs=pl.BlockSpec((group, cols, ids.shape[1]), lambda i: (0, 0, 0)),
        out_shape=jax.ShapeDtypeStruct((group, cols, ids.shape[1]), BF16),
        scratch_shapes=[pltpu.VMEM((cols, ids.shape[1]), F32)],
        compiler_params=params(),
        cost_estimate=cost(2 * cols * ent * 128, cols * ent * 2),
        name="pick_negs",
    )(ids, ent_t)


def up_to_here():
    rows = lax.broadcasted_iota(I32, (LANES, LANES), 0)
    cols = lax.broadcasted_iota(I32, (LANES, LANES), 1)
    return jnp.where(rows <= cols, 1.0, 0.0).astype(BF16)


def up_to_here():
    rows = lax.broadcasted_iota(I32, (LANES, LANES), 0)
    cols = lax.broadcasted_iota(I32, (LANES, LANES), 1)
    return jnp.where(rows <= cols, 1.0, 0.0).astype(BF16)


def band(rows, slots):
    bands = LANES // slots
    return rows if bands == 1 else pl.cdiv(pl.cdiv(rows, bands), 16) * 16


def pick_coef_kernel(nrel, fold, rel_ref, coef_ref, picked_ref, halves, acc):
    step = pl.program_id(0)
    nb, width = coef_ref.shape
    part = width // fold
    tall = acc.shape[0]
    half = tall // 2
    lane = lax.broadcasted_iota(I32, (nb, part), 1) + step * width
    spare = [jnp.zeros((half - nb, part), F32)] * (half > nb)
    for f in range(fold):
        block = coef_ref[:, f * part:(f + 1) * part]
        block = jnp.where(lane < nrel - f * part, block, 0.0)
        low = block - block.astype(BF16).astype(F32)
        both = jnp.concatenate([block, *spare, low, *spare], axis=0)
        halves[f * tall:(f + 1) * tall] = both.astype(BF16)
    here = rel_ref[...] - step * width
    where = here // part
    here = jnp.where((here >= 0) & (here < width), here - where * part, -1)
    found = nn(halves[...], hits(here, part, 0))
    total = jnp.where(where == 0, found[0:tall], 0.0)
    for f in range(1, fold):
        total = jnp.where(where == f, found[f * tall:(f + 1) * tall], total)

    @pl.when(step == 0)
    def _():
        acc[...] = total

    @pl.when(step > 0)
    def _():
        acc[...] += total

    @pl.when(step == pl.num_programs(0) - 1)
    def _():
        picked_ref[...] = acc[0:nb] + acc[half:half + nb]


def pick_coef(rel, coef_t):
    nb, nrel = coef_t.shape
    triples = rel.shape[1]
    fold = 4
    width = fold * 1920
    tall = 2 * (pl.cdiv(nb, 8) * 8)
    return pl.pallas_call(
        functools.partial(pick_coef_kernel, nrel, fold),
        grid=(pl.cdiv(nrel, width),),
        in_specs=[
            pl.BlockSpec((1, triples), lambda i: (0, 0)),
            pl.BlockSpec((nb, width), lambda i: (0, i)),
        ],
        out_specs=pl.BlockSpec((nb, triples), lambda i: (0, 0)),
        out_shape=jax.ShapeDtypeStruct((nb, triples), F32),
        scratch_shapes=[pltpu.VMEM((fold * tall, width // fold), BF16),
                        pltpu.VMEM((tall, triples), F32)],
        compiler_params=params(),
        cost_estimate=cost(2 * tall * nrel * triples, nb * nrel * 4),
        name="pick_coef",
    )(rel, coef_t)


def slot_of_relation(rel, devices, plan):
    span, slots, room = plan
    triples = rel.shape[1]
    number = lax.broadcasted_iota(I32, (devices, LANES), 0)
    later = lax.broadcasted_iota(I32, (LANES, triples), 1)
    row = lax.broadcasted_iota(I32, (LANES, triples), 0)
    seen = jnp.zeros((1, triples), F32)
    same = []
    for b in range(triples // LANES):
        down = jnp.broadcast_to(
            rel[:, b * LANES:(b + 1) * LANES].astype(F32), (LANES, LANES)).T[:, 0:1]
        equal = jnp.where(down.astype(I32) == rel, 1.0, 0.0)
        same.append(equal.astype(BF16))
        before = jnp.where(row + b * LANES < later, equal, 0.0)
        seen = seen + jnp.sum(before, axis=0, keepdims=True)
    first = jnp.where(seen == 0.0, 1.0, 0.0)
    summer = rel // span
    marks = []
    for b in range(triples // LANES):
        lanes = slice(b * LANES, (b + 1) * LANES)
        marks.append(jnp.where(number == summer[:, lanes], first[:, lanes], 0.0))
    sums = nn(jnp.concatenate(marks, axis=0).astype(BF16), up_to_here())
    carry = jnp.zeros((devices, 1), F32)
    lead = []
    for b, mark in enumerate(marks):
        part = sums[b * devices:(b + 1) * devices]
        lead.append(jnp.sum(mark * (part + carry - 1.0), axis=0, keepdims=True))
        carry = carry + part[:, LANES - 1:LANES]
    lead = jnp.minimum(jnp.concatenate(lead, axis=1), 255.0)
    lead = jnp.broadcast_to(lead, (16, triples)).astype(BF16)
    slot = nn(lead, jnp.concatenate(same, axis=0))[0:1].astype(I32)
    fits = slot < room
    place = jnp.where(fits, summer * slots + slot, -1)
    local = jnp.where(seen == 0.0, rel - summer * span, -1)
    over = jnp.max(jnp.where(fits, 0.0, 1.0), axis=1, keepdims=True)
    return place, local, over


def coef_blocks(rows, base, place, local, over, devices, plan, share):
    span, slots, room = plan
    nb = rows.shape[0]
    cols = base.shape[1]
    lanes = devices * slots

    def halves(block):
        spare = jnp.zeros((PAD - block.shape[0], block.shape[1]), F32)
        return jnp.concatenate(split(jnp.concatenate([block, spare], axis=0)), axis=0)

    high = local // 64
    pair = jnp.concatenate([high, local - high * 64], axis=0)
    pair = jnp.where(local >= 0, pair, 0).astype(F32)
    both = nt(halves(jnp.concatenate([rows, pair], axis=0)), hits(place, lanes, 0))
    column = lax.broadcasted_iota(I32, (1, cols), 1)
    owner = column // share
    spots = owner * slots + room + column - owner * share
    both = both + nt(halves(base), hits(spots, lanes, 0))
    row = lax.broadcasted_iota(I32, (PAD, lanes), 0)
    return jnp.where(row == nb + 2, over, both[0:PAD] + both[PAD:])


def score_kernel(neg_count, plan, share, rel_ref, picked_ref, negs_ref, head_ref, tail_ref,
                 row_ref, bases_ref, send_ref, grads_ref, rows_ref, base_ref, probs_ref, hrel_ref):
    group, cols, per = negs_ref.shape
    triples = head_ref.shape[1]
    devices, high, _ = send_ref.shape
    slots = plan[1]
    picked = picked_ref[...]
    vec = precise(nn, bases_ref[...], picked)
    head = head_ref[...].astype(F32)
    tail = tail_ref[...].astype(F32)
    head_vec = head * vec
    gate = jax.nn.sigmoid(-jnp.sum(head_vec * tail, axis=0, keepdims=True))
    head_rel = head_vec.astype(BF16)
    hrel_ref[...] = head_rel
    mix = jnp.zeros((cols, triples), F32)
    for first in range(0, group, 8):
        negs = jnp.concatenate([negs_ref[first + k] for k in range(8)], axis=1)
        probs = (0.5 * jnp.tanh(0.5 * tn(negs, head_rel)) + 0.5).astype(BF16)
        probs_ref[first * per:(first + 8) * per] = probs
        mix = mix + nn(negs, probs)
    rel_grad = -gate * head * tail + head * mix / neg_count
    rows = precise(nn, bases_ref[...].T, rel_grad)
    base = precise(nt, picked, rel_grad)
    rows_ref[...] = rows
    base_ref[...] = base
    place, local, over = slot_of_relation(rel_ref[...], devices, plan)
    both = coef_blocks(rows, base, place, local, over, devices, plan, share)
    bands = LANES // slots
    if bands * high > PAD:
        spare = jnp.zeros((bands * high - PAD, both.shape[1]), F32)
        both = jnp.concatenate([both, spare], axis=0)
    for o in range(devices):
        block = [both[b * high:(b + 1) * high, o * slots:(o + 1) * slots] for b in range(bands)]
        send_ref[o] = jnp.concatenate(block, axis=1).astype(BF16)
    grads_ref[0:cols, 0:triples] = (-gate * vec * tail + vec * mix / neg_count).astype(BF16)
    grads_ref[0:cols, triples:] = (-gate * head * vec).astype(BF16)
    for side in range(2):
        ids = row_ref[side:side + 1]
        lanes = slice(side * triples, (side + 1) * triples)
        upper = ids // 64
        pair = jnp.concatenate([upper, ids - upper * 64], axis=0).astype(F32)
        more = grads_ref.shape[0] - cols - 2
        if more:
            pair = jnp.concatenate([pair, jnp.zeros((more, triples), F32)], axis=0)
        grads_ref[cols:, lanes] = pair.astype(BF16)


def score_step(rel, picked, negs, head_t, tail_t, rows, bases_t, tall, neg_count, devices, plan,
               share):
    group, cols, per = negs.shape
    triples = head_t.shape[1]
    nb = bases_t.shape[1]
    high = pl.cdiv(PAD * plan[1], 8 * LANES) * 8
    outs = [((devices, high, LANES), BF16), ((tall, 2 * triples), BF16), ((nb, triples), F32),
            ((nb, cols), F32), ((group * per, triples), BF16), ((cols, triples), BF16)]
    return pl.pallas_call(
        functools.partial(score_kernel, neg_count, plan, share),
        out_shape=[jax.ShapeDtypeStruct(s, d) for s, d in outs],
        compiler_params=params(),
        cost_estimate=cost(2 * cols * triples * 2 * group * per, 16 << 20),
        name="score_step",
    )(rel, picked, negs, head_t, tail_t, rows, bases_t)


def order_kernel(devices, slots, grads_ref, owner_ref, send_ref, pos):
    owners, high, _ = send_ref.shape
    bands = LANES // slots
    step = pl.program_id(0)

    @pl.when(step == 0)
    def _():
        owner = owner_ref[...]
        triples = owner.shape[1]
        number = lax.broadcasted_iota(I32, (devices, LANES), 0)
        parts, marks = [], []
        for side in range(2):
            for b in range(triples // LANES):
                part = owner[side:side + 1, b * LANES:(b + 1) * LANES]
                parts.append(part)
                marks.append(jnp.where(number == part, 1.0, 0.0))
        sums = nn(jnp.concatenate(marks, axis=0).astype(BF16), up_to_here())
        carry = jnp.zeros((devices, 1), F32)
        for b, (part, mark) in enumerate(zip(parts, marks)):
            here = sums[b * devices:(b + 1) * devices]
            slot = jnp.sum(mark * (here + carry), axis=0, keepdims=True) - 1.0
            pos[:, b * LANES:(b + 1) * LANES] = part * slots + slot.astype(I32)
            carry = carry + here[:, LANES - 1:LANES]

    part = nt(grads_ref[...], hits(pos[...], owners * slots, step * owners * slots))
    part = part.astype(BF16)
    for o in range(owners):
        at = o * slots
        block = [part[b * high:(b + 1) * high, at:at + slots] for b in range(bands)]
        send_ref[o] = jnp.concatenate(block, axis=1)


def order_slots(grads, owner_t, devices, slots, rows):
    owners = 512 // slots
    high = band(rows, slots)
    whole = lambda shape: pl.BlockSpec(shape, lambda i: (0,) * len(shape))
    return pl.pallas_call(
        functools.partial(order_kernel, devices, slots),
        grid=(devices // owners,),
        in_specs=[whole(grads.shape), whole(owner_t.shape)],
        out_specs=pl.BlockSpec((owners, high, LANES), lambda i: (i, 0, 0)),
        out_shape=jax.ShapeDtypeStruct((devices, high, LANES), BF16),
        scratch_shapes=[pltpu.VMEM((1, grads.shape[1]), I32)],
        compiler_params=params(),
        cost_estimate=cost(rows * grads.shape[1] * devices * slots * 2, 4 << 20),
        name="order_slots",
    )(grads, owner_t)


def partial_kernel(neg_count, me_ref, probs_ref, hrel_ref, parts_ref, block):
    half, per = parts_ref.shape[1], parts_ref.shape[3]
    for first in range(0, 2 * half, 8):
        part = nt(hrel_ref[...], probs_ref[first * per:(first + 8) * per]) / neg_count
        block[...] = part
        for k in range(8):
            lane = pl.multiple_of((k ^ me_ref[0]) * per, per)
            parts_ref[k % 2, (first + k) // 2] = block[:, pl.ds(lane, per)].astype(BF16)


def partial_step(me, probs, hrel, group, neg_count):
    cols = hrel.shape[0]
    whole = lambda shape: pl.BlockSpec(shape, lambda i, me: (0,) * len(shape))
    shape = (2, group // 2, cols, LANES)
    return pl.pallas_call(
        functools.partial(partial_kernel, neg_count),
        grid_spec=pltpu.PrefetchScalarGridSpec(
            num_scalar_prefetch=1,
            grid=(1,),
            in_specs=[whole(probs.shape), whole(hrel.shape)],
            out_specs=whole(shape),
            scratch_shapes=[pltpu.VMEM((cols, 8 * LANES), F32)],
        ),
        out_shape=jax.ShapeDtypeStruct(shape, BF16),
        compiler_params=params(),
        cost_estimate=cost(1, 1),
        name="partial_step",
    )(me, probs, hrel)


def coef_sum_kernel(nb, plan, recv_ref, out_ref, flag_ref, left):
    span, slots, room = plan
    sources, high, _ = recv_ref.shape
    bands = LANES // slots
    for s in range(0, sources, bands):
        lanes = slice(s * slots, (s + bands) * slots)
        tall = []
        for b in range(bands):
            block = [recv_ref[s + k, :, b * slots:(b + 1) * slots] for k in range(bands)]
            tall.append(jnp.concatenate(block, axis=1).astype(F32))
        left[:, lanes] = jnp.concatenate(tall, axis=0)[0:PAD].astype(BF16)
    extra = left[PAD - 16:PAD].astype(F32)
    at = nb - (PAD - 16)
    ids = (extra[at:at + 1] * 64.0 + extra[at + 1:at + 2]).astype(I32)
    lane = lax.broadcasted_iota(I32, ids.shape, 1)
    lane = lane - lane // slots * slots
    ids = jnp.where(lane < room, ids, span + lane - room)
    total = nt(left[0:PAD], hits(ids, out_ref.shape[1], 0))
    out_ref[...] = total[0:nb].astype(BF16)
    over = jnp.max(extra[at + 2:at + 3], axis=1, keepdims=True)
    flag_ref[...] = jnp.broadcast_to(over, flag_ref.shape).astype(I32)


def coef_sum(recv, nb, plan, width):
    sources = recv.shape[0]
    slots = plan[1]
    return pl.pallas_call(
        functools.partial(coef_sum_kernel, nb, plan),
        out_shape=[jax.ShapeDtypeStruct((nb, width), BF16), jax.ShapeDtypeStruct((1, LANES), I32)],
        scratch_shapes=[pltpu.VMEM((PAD, sources * slots), BF16)],
        compiler_params=params(20),
        cost_estimate=cost(1, 1),
        name="coef_sum",
    )(recv)


def spread_kernel(span, share, place_ref, *refs):
    sets, (coef_ref, base_ref, pieces, strips) = refs[:-4], refs[-4:]
    step = pl.program_id(0)
    group, layers, nb, _ = pieces.shape

    @pl.when(step == 0)
    def _():
        number = 0
        for ref in sets:
            for s in range(ref.shape[0]):
                pieces[number ^ place_ref[0]] = ref[s]
                number += 1

    slab = lax.rem(place_ref[1] - step + layers, layers)
    row = [pieces[k, slab].astype(F32) for k in range(group)]
    coef_ref[...] = jnp.concatenate([r[:, 0:span] for r in row], axis=1)
    strip = jnp.concatenate([r[:, span:span + share] for r in row], axis=1)
    strips[step] = jnp.concatenate([strip, jnp.zeros((PAD - nb, strip.shape[1]), F32)], axis=0)

    @pl.when(step == layers - 1)
    def _():
        whole = jnp.concatenate([strips[g] for g in range(layers)], axis=1)
        base_ref[...] = whole[0:nb, 0:base_ref.shape[0]].T


def spread(me, layer, sets, span, share, nrel, cols):
    group = sum(s.shape[0] for s in sets)
    _, layers, nb, width = sets[0].shape
    whole = lambda shape: pl.BlockSpec(shape, lambda i, place: (0,) * len(shape))
    return pl.pallas_call(
        functools.partial(spread_kernel, span, share),
        grid_spec=pltpu.PrefetchScalarGridSpec(
            num_scalar_prefetch=1,
            grid=(layers,),
            in_specs=[whole(s.shape) for s in sets],
            out_specs=[
                pl.BlockSpec((nb, group * span), lambda i, place: (0, i)),
                whole((cols, nb)),
            ],
            scratch_shapes=[pltpu.VMEM((group, layers, nb, width), BF16),
                            pltpu.VMEM((layers, PAD, group * share), F32)],
        ),
        out_shape=[jax.ShapeDtypeStruct((nb, nrel), F32), jax.ShapeDtypeStruct((cols, nb), F32)],
        compiler_params=params(),
        cost_estimate=cost(1, 1),
        name="spread",
    )(jnp.concatenate([me, layer]), *sets)


def add_rows_kernel(slots, recv_ref, neg_ref, own_ref, out_ref, grads, ids, sems):
    step = pl.program_id(0)
    cols, width = out_ref.shape
    sources, high, _ = recv_ref.shape
    bands = LANES // slots
    lanes = sources * slots

    @pl.when(step == 0)
    def _():
        copies = []
        if bands == 1:
            for s in range(sources):
                to = grads.at[:, s * slots:(s + 1) * slots]
                copies.append(pltpu.make_async_copy(recv_ref.at[s], to, sems.at[s]))
        else:
            for s in range(0, sources, bands):
                at = slice(s * slots, (s + bands) * slots)
                for b in range(bands):
                    block = [recv_ref[s + k, :, b * slots:(b + 1) * slots] for k in range(bands)]
                    grads[b * high:(b + 1) * high, at] = jnp.concatenate(block, axis=1)
        for copy in copies:
            copy.start()
        top, low = split(own_ref[...])
        grads[0:cols, lanes:lanes + LANES] = top
        grads[0:cols, lanes + LANES:] = low
        ids[:, lanes:lanes + LANES] = neg_ref[...]
        ids[:, lanes + LANES:] = neg_ref[...]
        for copy in copies:
            copy.wait()
        pair = grads[cols:cols + 2, 0:lanes].astype(F32)
        ids[:, 0:lanes] = (pair[0:1] * 64.0 + pair[1:2]).astype(I32)

    out_ref[...] = nt(grads[0:cols], hits(ids[...], width, step * width))


def add_rows(recv, slots, cols, ent, neg_ids, own_neg):
    sources, high, _ = recv.shape
    bands = LANES // slots
    width = 1024
    lanes = sources * slots + 2 * LANES
    whole = lambda shape: pl.BlockSpec(shape, lambda i: (0,) * len(shape))
    there = pl.BlockSpec(memory_space=pl.ANY) if bands == 1 else whole(recv.shape)
    return pl.pallas_call(
        functools.partial(add_rows_kernel, slots),
        grid=(ent // width,),
        in_specs=[there, whole(neg_ids.shape), whole(own_neg.shape)],
        out_specs=pl.BlockSpec((cols, width), lambda i: (0, i)),
        out_shape=jax.ShapeDtypeStruct((cols, ent), F32),
        scratch_shapes=[pltpu.VMEM((bands * high, lanes), BF16),
                        pltpu.VMEM((1, lanes), I32),
                        pltpu.SemaphoreType.DMA((sources,))],
        compiler_params=params(32),
        cost_estimate=cost(1, 1),
        name="add_rows",
    )(recv, neg_ids, own_neg)


def from_group(block, pairs, group):
    block = block[None]
    if group != 8:
        parts = lax.all_to_all(pairs, "dev", 0, 0, tiled=True)
        return [lax.all_gather(block, "dev", axis=0, tiled=True)], [parts]
    swap = lambda x, far: lax.ppermute(x, "dev", [(i, i ^ far) for i in range(group)])
    even = [block] + [swap(block, far) for far in (2, 4, 6)]
    parts = [pairs[0:1]] + [swap(pairs[n:n + 1], 2 * n) for n in (1, 2, 3)]
    even, parts = lax.optimization_barrier((even, parts))
    return [b for e in even for b in (e, swap(e, 1))], parts


def sum_pairs(parts, group):
    if group != 8:
        return parts.swapaxes(0, 1).reshape((group,) + parts.shape[2:])
    near = lax.ppermute(parts[1], "dev", [(i, i ^ 1) for i in range(group)])
    return (parts[0].astype(F32) + near.astype(F32)).astype(BF16)


def shift_layers(block, far, layers):
    return lax.ppermute(block, "grp", [(i, (i + far) % layers) for i in range(layers)])


def everywhere(values):
    for axis in ("dev", "grp"):
        count = lax.axis_size(axis)
        assert count & (count - 1) == 0
        far = 1
        while far < count:
            swap = [(i, i ^ far) for i in range(count)]
            values = tuple(v + lax.ppermute(v, axis, swap) for v in values)
            far *= 2
    return values


def per_device(head_emb, tail_emb, relation, owners, owner_rows, entities, neg_rows, coef, bases):
    triples, cols = head_emb.shape
    group = lax.axis_size("dev")
    layers = lax.axis_size("grp")
    devices = layers * group
    neg_count = neg_rows.shape[1] * group
    ent_local = entities.shape[0]
    nrel, nb = coef.shape
    cap = 4 * triples // devices
    tall = LANES // cap * band(cols + 2, cap)
    share = pl.cdiv(cols, devices)
    step = LANES // math.gcd(group, LANES)
    span = pl.cdiv(pl.cdiv(nrel, devices), step) * step
    slots = 2 * triples // devices
    plan = (span, slots, slots - share)
    width = pl.cdiv(span + share, LANES) * LANES

    head_t, tail_t, owner_t, row_t = head_emb.T, tail_emb.T, owners.T, owner_rows.T
    coef_t, bases_t = coef.T, bases.T
    rel = relation.reshape(1, triples)

    sent_negs = pick_negs(neg_rows, entities.T, group)
    negs = lax.all_to_all(sent_negs, "dev", 0, 0, tiled=True)
    picked = pick_coef(rel, coef_t)
    coef_send, grads, rows, base, probs, hrel = score_step(
        rel, picked, negs, head_t, tail_t, row_t, bases_t, tall, neg_count, devices, plan, share)
    coef_recv = lax.all_to_all(coef_send, ("grp", "dev"), 0, 0, tiled=True)
    send = order_slots(grads, owner_t, devices, cap, cols + 2)
    send, coef_recv = lax.optimization_barrier((send, coef_recv))
    piece, flag = coef_sum(coef_recv, nb, plan, width)
    slabs = [piece] + [shift_layers(piece, far, layers) for far in range(1, layers)]
    me = lax.axis_index("dev").astype(I32).reshape(1)
    layer = lax.axis_index("grp").astype(I32).reshape(1)
    at = me if group == 8 else jnp.zeros((1,), I32)
    send, slabs = lax.optimization_barrier((send, slabs))
    recv = lax.all_to_all(send, ("grp", "dev"), 0, 0, tiled=True)
    pairs = sum_pairs(partial_step(at, probs, hrel, group, neg_count), group)
    pieces, parts = from_group(jnp.stack(slabs), pairs, group)
    own_neg = sum(part.astype(F32).sum(axis=0) for part in parts)
    pieces, own_neg = lax.optimization_barrier((pieces, own_neg))

    def packed():
        return tuple(spread(at, layer, pieces, span, share, nrel, cols))

    def dense():
        return everywhere((jnp.zeros((nb, nrel), F32).at[:, relation].add(rows), base.T))

    coef_grad, bases_grad = lax.cond(flag[0, 0] == 0, packed, dense)
    ent_grad = add_rows(recv, cap, cols, ent_local, neg_rows, own_neg)
    return ent_grad.T, coef_grad.T, bases_grad.T


def solution(mesh):
    return jax.shard_map(
        per_device,
        mesh=mesh,
        in_specs=(
            P(("grp", "dev"), None),
            P(("grp", "dev"), None),
            P(("grp", "dev")),
            P(("grp", "dev"), None),
            P(("grp", "dev"), None),
            P(("grp", "dev"), None),
            P(None, ("grp", "dev")),
            P(),
            P(),
        ),
        out_specs=(P(("grp", "dev"), None), P(), P()),
        check_vma=False,
    )
```
